128 devices in a mesh: rows: 32 (over x, y, z_lo), seq: 4 (over z_hi, core).
Axes of the slice: x: 4, y: 4, z: 4 (z_hi: 2, z_lo: 2; z = z_hi * 2 + z_lo), core: 2. Of those that a mesh axis runs over, the one named last changes fastest.
Arguments:
- image: bfloat16 [256, 256, 256], P('rows', 'seq'), may hold values from -42 to 42
- gain_attn: float32 [256], replicated, may hold values from 0.1 to 1.9
- w_qkv_fine: bfloat16 [256, 768], replicated, may hold values from -0.375 to 0.375
- scale_fine: float32 [4], replicated, may hold values from 8 to 40
- w_out_fine: bfloat16 [256, 256], replicated, may hold values from -1.5 to 1.5
- gain_ffn: float32 [256], replicated, may hold values from 0.1 to 1.9
- w_ffn_in: bfloat16 [256, 1536], replicated, may hold values from -0.375 to 0.375
- w_ffn_out: bfloat16 [768, 256], replicated, may hold values from -0.4375 to 0.4375
- w_merge: bfloat16 [1024, 1024], replicated, may hold values from -0.1875 to 0.1875
- gain_coarse: float32 [1024], replicated, may hold values from 0.1 to 1.9
- w_qkv_coarse: bfloat16 [1024, 3072], replicated, may hold values from -0.1875 to 0.1875
- scale_coarse: float32 [16], replicated, may hold values from 24 to 48
- w_out_coarse: bfloat16 [1024, 1024], replicated, may hold values from -0.75 to 0.75
Outputs:
- fine_out: bfloat16 [256, 256, 256], P('rows', 'seq')
- coarse_out: bfloat16 [128, 128, 1024], P('rows', 'seq')
The draws below stay inside these ranges and needn't reach their ends.
All inputs are finite; a program needn't handle non-finite values.
Results may differ from the reference program's by a relative error of at most 0.025.
The reference program's roundings to bfloat16 on the way count: a program that leaves them out, or rounds other values in their place, can miss the bound.
Values may be sent and summed in bfloat16 or wider, within the bound.
A program may use at most 128 MiB of HBM per device.

```python
import math
import jax
import jax.numpy as jnp
from jax import lax

D_FINE = 256
FF_FINE = 768
D_COARSE = 1024
HEAD = 64
HEADS_FINE = 4
HEADS_COARSE = 16
FROWS = 256
FCOLS = 256


def draw_image(key, part):
    key = jax.random.fold_in(key, 11)
    base_key, row_key, chan_key = jax.random.split(key, 3)
    row_scale = jnp.exp(jax.random.uniform(row_key, (FROWS, FCOLS, 1), minval=-1.15, maxval=1.15))
    chan_scale = jnp.exp(jax.random.uniform(chan_key, (1, 1, D_FINE), minval=-1.15, maxval=1.15))
    base = jnp.clip(jax.random.normal(base_key, (FROWS, FCOLS, D_FINE)), -4.0, 4.0)
    return (base * row_scale * chan_scale).astype(jnp.bfloat16)


def centred(rng, extent, deviation, limit, kind=jnp.bfloat16):
    array = deviation * jax.random.normal(rng, extent, jnp.float32)
    return jnp.clip(array, min=-limit, max=limit).astype(kind)


def setup_inputs(seed: int = 0) -> dict:
    seeds = jax.random.split(jax.random.key(seed), 14)
    image = draw_image(jax.random.fold_in(seeds[13], 71), 0)
    gain_attn = jnp.clip(1.0 + 0.18 * jax.random.normal(seeds[1], (D_FINE,), jnp.float32), 0.1, 1.9)
    w_qkv_fine = centred(seeds[2], (D_FINE, 3 * D_FINE), D_FINE ** -0.5, 0.375)
    scale_fine = jnp.clip(jnp.exp(jax.random.uniform(seeds[3], (HEADS_FINE,), jnp.float32, math.log(8.0), math.log(40.0))), 8.0, 40.0)
    w_out_fine = centred(seeds[4], (D_FINE, D_FINE), (D_FINE // 16) ** -0.5, 1.5)
    gain_ffn = jnp.clip(1.0 + 0.18 * jax.random.normal(seeds[5], (D_FINE,), jnp.float32), 0.1, 1.9)
    w_ffn_in = centred(seeds[6], (D_FINE, 2 * FF_FINE), D_FINE ** -0.5, 0.375)
    w_ffn_out = centred(seeds[7], (FF_FINE, D_FINE), (FF_FINE // 4) ** -0.5, 0.4375)
    w_merge = centred(seeds[8], (4 * D_FINE, D_COARSE), (4 * D_FINE) ** -0.5, 0.1875)
    gain_coarse = jnp.clip(1.0 + 0.18 * jax.random.normal(seeds[9], (D_COARSE,), jnp.float32), 0.1, 1.9)
    w_qkv_coarse = centred(seeds[10], (D_COARSE, 3 * D_COARSE), D_COARSE ** -0.5, 0.1875)
    scale_coarse = jnp.clip(jnp.exp(jax.random.uniform(seeds[11], (HEADS_COARSE,), jnp.float32, math.log(24.0), math.log(48.0))), 24.0, 48.0)
    w_out_coarse = centred(seeds[12], (D_COARSE, D_COARSE), (D_COARSE // 16) ** -0.5, 0.75)
    return {"image": image, "gain_attn": gain_attn, "w_qkv_fine": w_qkv_fine, "scale_fine": scale_fine, "w_out_fine": w_out_fine, "gain_ffn": gain_ffn, "w_ffn_in": w_ffn_in, "w_ffn_out": w_ffn_out, "w_merge": w_merge, "gain_coarse": gain_coarse, "w_qkv_coarse": w_qkv_coarse, "scale_coarse": scale_coarse, "w_out_coarse": w_out_coarse}


def rms_scaled(values, gain):
    mean_square = lax.optimization_barrier(jnp.mean(values * values, axis=-1, keepdims=True))
    return values * lax.rsqrt(mean_square + 1e-06) * gain

def unit_heads(values, head_count):
    shaped = values.astype(jnp.float32).reshape(values.shape[:-1] + (head_count, HEAD))
    mean_square = lax.optimization_barrier(jnp.mean(shaped * shaped, axis=-1, keepdims=True))
    return (shaped * lax.rsqrt(mean_square + 1e-06)).astype(jnp.bfloat16)

def neighbour(projected, scale_fine):
    grid_rows, grid_cols, triple = projected.shape
    width = triple // 3
    head_count = width // HEAD
    queries = unit_heads(projected[:, :, :width], head_count).astype(jnp.float32)
    key_unit = unit_heads(projected[:, :, width:2 * width], head_count)
    values = projected[:, :, 2 * width:].reshape(grid_rows, grid_cols, head_count, HEAD)
    margin = ((3, 3), (3, 3), (0, 0), (0, 0))
    padded_keys = jnp.pad(key_unit, margin)
    padded_values = jnp.pad(values, margin)
    row_index = jnp.arange(grid_rows)[:, None]
    col_index = jnp.arange(grid_cols)[None, :]
    factor = scale_fine / HEAD
    numerator = jnp.zeros((grid_rows, grid_cols, head_count, HEAD), jnp.float32)
    denominator = jnp.zeros((grid_rows, grid_cols, head_count), jnp.float32)
    for row_shift in range(7):
        for col_shift in range(7):
            shifted = padded_keys[row_shift:row_shift + grid_rows, col_shift:col_shift + grid_cols].astype(jnp.float32)
            scores = lax.optimization_barrier(jnp.sum(queries * shifted, axis=-1)) * factor
            source_row = row_index + row_shift - 3
            source_col = col_index + col_shift - 3
            inside = (source_row >= 0) & (source_row < grid_rows) & (source_col >= 0) & (source_col < grid_cols)
            weights = jnp.where(inside[:, :, None], jnp.exp(scores), 0.0)
            denominator = denominator + weights
            rounded = lax.optimization_barrier(weights.astype(jnp.bfloat16)).astype(jnp.float32)
            moved_values = padded_values[row_shift:row_shift + grid_rows, col_shift:col_shift + grid_cols].astype(jnp.float32)
            numerator = numerator + rounded[..., None] * moved_values
    return (numerator / denominator[..., None]).astype(jnp.bfloat16).reshape(grid_rows, grid_cols, width)

def feed_forward(stream_rows, gain_ffn, w_ffn_in, w_ffn_out):
    hidden_units = w_ffn_out.shape[0]
    normed_ffn = rms_scaled(stream_rows, gain_ffn).astype(jnp.bfloat16)
    mixed = jnp.dot(normed_ffn, w_ffn_in, preferred_element_type=jnp.float32)
    gated = (mixed[:, :hidden_units] * jax.nn.gelu(mixed[:, hidden_units:])).astype(jnp.bfloat16)
    return (stream_rows + jnp.dot(gated, w_ffn_out, preferred_element_type=jnp.float32)).astype(jnp.bfloat16)

def reference(image, gain_attn, w_qkv_fine, scale_fine, w_out_fine, gain_ffn, w_ffn_in, w_ffn_out, w_merge, gain_coarse, w_qkv_coarse, scale_coarse, w_out_coarse):
    grid_rows, grid_cols, width = image.shape
    stream = image.astype(jnp.float32)
    normed = rms_scaled(stream, gain_attn).astype(jnp.bfloat16)
    projected = jnp.dot(normed.reshape(-1, width), w_qkv_fine, preferred_element_type=jnp.float32).astype(jnp.bfloat16)
    projected = projected.reshape(grid_rows, grid_cols, 3 * width)
    attended = neighbour(projected, scale_fine)
    stream = stream.reshape(-1, width) + jnp.dot(attended.reshape(-1, width), w_out_fine, preferred_element_type=jnp.float32)
    token_rows = stream.shape[0]
    block_rows = math.gcd(token_rows, 16384)
    blocked = stream.reshape(token_rows // block_rows, block_rows, width)
    fine_out = lax.map(lambda rows_block: feed_forward(rows_block, gain_ffn, w_ffn_in, w_ffn_out), blocked)
    fine_out = fine_out.reshape(grid_rows, grid_cols, width)
    merged = fine_out.reshape(grid_rows // 2, 2, grid_cols // 2, 2, width).transpose(0, 2, 1, 3, 4).reshape(-1, 4 * width)
    coarse_in = jnp.dot(merged, w_merge, preferred_element_type=jnp.float32).astype(jnp.bfloat16)
    token_total, coarse_width = coarse_in.shape
    head_total = coarse_width // HEAD
    coarse_stream = coarse_in.astype(jnp.float32)
    normed_coarse = rms_scaled(coarse_stream, gain_coarse).astype(jnp.bfloat16)
    triple = jnp.dot(normed_coarse, w_qkv_coarse, preferred_element_type=jnp.float32).astype(jnp.bfloat16)
    query_unit = unit_heads(triple[:, :coarse_width], head_total).transpose(1, 0, 2)
    key_unit = unit_heads(triple[:, coarse_width:2 * coarse_width], head_total).transpose(1, 0, 2)
    value_part = triple[:, 2 * coarse_width:].reshape(token_total, head_total, HEAD).transpose(1, 0, 2)
    block_size = math.gcd(token_total, 1024)

    def per_head(inputs):
        head_queries, head_keys, head_values, factor = inputs

        def per_block(block_queries):
            scores = jnp.dot(block_queries, head_keys.T, preferred_element_type=jnp.float32) * factor
            weights = jnp.exp(scores)
            weight_sum = lax.optimization_barrier(jnp.sum(weights, axis=-1))
            numerator = jnp.dot(weights.astype(jnp.bfloat16), head_values, preferred_element_type=jnp.float32)
            return (numerator / weight_sum[:, None]).astype(jnp.bfloat16)
        return lax.map(per_block, head_queries.reshape(-1, block_size, HEAD)).reshape(-1, HEAD)
    attended_coarse = lax.map(per_head, (query_unit, key_unit, value_part, scale_coarse / HEAD))
    attended_coarse = attended_coarse.transpose(1, 0, 2).reshape(token_total, coarse_width)
    coarse_out = (coarse_stream + jnp.dot(attended_coarse, w_out_coarse, preferred_element_type=jnp.float32)).astype(jnp.bfloat16)
    return (fine_out, coarse_out.reshape(grid_rows // 2, grid_cols // 2, coarse_width))
```

```python
import functools
import math

import jax
import jax.numpy as jnp
from jax import lax
from jax.experimental import pallas as pl
from jax.experimental.pallas import tpu as pltpu
from jax.sharding import PartitionSpec as P

HEAD = 64
MESH = pl.DeviceIdType.MESH
BF = jnp.bfloat16
F32 = jnp.float32
LOG2E = math.log2(math.e)

FR, FC, FD = 8, 64, 256
PR, PC = FR + 6, FC + 32
CT, CD = 128, 1024
NHEAD = 16
CHUNK = NHEAD * CT
VMEM_LIMIT = 56 * 2**20


def rms(values, gain):
    mean_square = jnp.mean(values * values, axis=-1, keepdims=True)
    return (values * lax.rsqrt(mean_square + 1e-06) * gain).astype(BF)


def head_blocks(width):
    row = lax.broadcasted_iota(jnp.int32, (width, width), 0) >> 6
    col = lax.broadcasted_iota(jnp.int32, (width, width), 1) >> 6
    return jnp.where(row == col, 1.0 / HEAD, 0.0).astype(BF)


def unit(values, blocks):
    width = blocks.shape[0]
    parts = []
    for start in range(0, values.shape[1], width):
        part = values[:, start : start + width]
        square = part * part
        high = square.astype(BF)
        low = (square - high.astype(F32)).astype(BF)
        mean = jnp.dot(high, blocks, preferred_element_type=F32) + jnp.dot(
            low, blocks, preferred_element_type=F32
        )
        parts.append(part * lax.rsqrt(mean + 1e-06))
    return parts[0] if len(parts) == 1 else jnp.concatenate(parts, axis=1)


def fine_kernel(
    image,
    gain_attn,
    w_qkv,
    scale_fine,
    w_out,
    gain_ffn,
    w_in_hbm,
    w_ffn_hbm,
    w_merge_hbm,
    gain_coarse,
    w_coarse_hbm,
    fine_out,
    coarse_in,
    kv_msg,
    q_msg,
    xpad,
    keys,
    vals,
    bias,
    attended,
    merged,
    w_in,
    w_ffn,
    w_merge,
    w_coarse,
    load_sem,
    send_sem,
    recv_sem,
):
    row, seq = lax.axis_index("rows"), lax.axis_index("seq")
    n_rows, n_seq = lax.axis_size("rows"), lax.axis_size("seq")

    loads = [
        pltpu.make_async_copy(image, xpad.at[pl.ds(3, FR), pl.ds(0, FC)], load_sem.at[0]),
        pltpu.make_async_copy(w_in_hbm, w_in, load_sem.at[1]),
        pltpu.make_async_copy(w_ffn_hbm, w_ffn, load_sem.at[2]),
        pltpu.make_async_copy(w_merge_hbm, w_merge, load_sem.at[3]),
        pltpu.make_async_copy(w_coarse_hbm, w_coarse, load_sem.at[4]),
    ]
    loads[0].start()

    barrier = pltpu.get_barrier_semaphore()
    around = [(dr, ds) for dr in (-1, 0, 1) for ds in (-1, 0, 1) if (dr, ds) != (0, 0)]
    for dr, ds in around:
        there = (lax.rem(row + dr + n_rows, n_rows), lax.rem(seq + ds + n_seq, n_seq))
        pl.semaphore_signal(barrier, inc=1, device_id=there, device_id_type=MESH)
    pl.semaphore_wait(barrier, len(around))

    source_rows = {-1: pl.ds(0, 3), 0: pl.ds(0, FR), 1: pl.ds(FR - 3, 3)}
    source_cols = {-1: pl.ds(0, 16), 0: pl.ds(0, FC), 1: pl.ds(FC - 16, 16)}
    target_rows = {-1: pl.ds(FR + 3, 3), 0: pl.ds(3, FR), 1: pl.ds(0, 3)}
    target_cols = {-1: pl.ds(FC + 16, 16), 0: pl.ds(0, FC), 1: pl.ds(FC, 16)}
    sends = []
    for i, (dr, ds) in enumerate(around):
        there = (lax.rem(row + dr + n_rows, n_rows), lax.rem(seq + ds + n_seq, n_seq))
        copy = pltpu.make_async_remote_copy(
            src_ref=image.at[source_rows[dr], source_cols[ds]],
            dst_ref=xpad.at[target_rows[dr], target_cols[ds]],
            send_sem=send_sem.at[i],
            recv_sem=recv_sem.at[i],
            device_id=there,
            device_id_type=MESH,
        )
        copy.start()
        sends.append(copy)
    for load in loads[1:]:
        load.start()

    query_col = lax.broadcasted_iota(jnp.int32, (FC, PC), 0)
    slot = lax.broadcasted_iota(jnp.int32, (FC, PC), 1)
    key_col = jnp.where(slot < FC, slot, jnp.where(slot < FC + 16, slot - FC - 16, slot - 16))
    gap = key_col - query_col
    near = jnp.where((gap >= -3) & (gap <= 3), 0.0, -1e30).astype(F32)
    bias[...] = jnp.concatenate([jnp.concatenate([near] * 7, axis=1)] * 4, axis=0)
    blocks = head_blocks(FD)
    gain = gain_attn[...]

    loads[0].wait()
    for copy in sends:
        copy.wait()

    pair = 2 * PC
    slot_col = lax.broadcasted_iota(jnp.int32, (pair, 1), 0)
    local_row = (slot_col >= PC).astype(jnp.int32)
    slot_col = slot_col - local_row * PC
    left_out = (slot_col >= FC) & (slot_col < FC + 16) & (seq == 0)
    right_out = (slot_col >= FC + 16) & (seq == n_seq - 1)

    def project(i, carry):
        normed = rms(xpad[pl.ds(i * 2, 2)].reshape(pair, FD).astype(F32), gain)
        kv = jnp.dot(normed, w_qkv[:, FD:], preferred_element_type=F32).astype(BF)
        start = pl.multiple_of(i * pair, pair)
        keys[pl.ds(start, pair), :] = unit(kv[:, :FD].astype(F32), blocks).astype(BF)
        global_row = row * FR + i * 2 + local_row - 3
        valid = (global_row >= 0) & (global_row < n_rows * FR)
        inside = jnp.where(valid & jnp.logical_not(left_out) & jnp.logical_not(right_out), 1.0, 0.0)
        value = jnp.concatenate(
            [kv[:, FD:].astype(F32) * inside, jnp.broadcast_to(inside, (pair, 128))], axis=1
        )
        vals[pl.ds(start, pair), :] = value.astype(BF)
        return carry

    lax.fori_loop(0, PR // 2, project, 0)

    lane_head = lax.broadcasted_iota(jnp.int32, (FC, FD), 1) >> 6
    factor = jnp.concatenate(
        [jnp.full((FC, 1), scale_fine[0, h] * (LOG2E / HEAD), F32) for h in range(4)], axis=0
    )

    def attend(r, carry):
        normed = rms(xpad[r + 3, 0:FC].astype(F32), gain)
        query = jnp.dot(normed, w_qkv[:, :FD], preferred_element_type=F32).astype(BF)
        query = unit(query.astype(F32), blocks)
        stacked = jnp.concatenate(
            [jnp.where(lane_head == h, query, 0.0).astype(BF) for h in range(4)], axis=0
        )
        window = pl.ds(pl.multiple_of(r * PC, PC), 7 * PC)
        scores = lax.dot_general(
            stacked, keys[window, :], (((1,), (1,)), ((), ())), preferred_element_type=F32
        )
        weights = jnp.exp2(scores * factor + bias[...]).astype(BF)
        total = jnp.dot(weights, vals[window, :], preferred_element_type=F32)
        inverse = 1.0 / total[:, FD:]
        scaled = total[:, :FD] * jnp.concatenate([inverse, inverse], axis=1)
        picked = jnp.where(lane_head == 0, scaled[:FC], 0.0)
        for h in range(1, 4):
            picked = jnp.where(lane_head == h, scaled[h * FC : (h + 1) * FC], picked)
        attended[pl.ds(pl.multiple_of(r * FC, FC), FC), :] = picked.astype(BF)
        return carry

    lax.fori_loop(0, FR, attend, 0)

    loads[1].wait()
    loads[2].wait()
    hidden = w_ffn.shape[0]
    take = lax.broadcasted_iota(jnp.int32, (128, 128), 0)
    come = lax.broadcasted_iota(jnp.int32, (128, 128), 1)
    wanted = (take >> 6) * 64 + (take & 31) * 2 + ((take >> 5) & 1)
    permute = jnp.where(come == wanted, 1.0, 0.0).astype(BF)
    gain_f = gain_ffn[...]

    def feed(i, carry):
        tokens = pl.ds(pl.multiple_of(i * 128, 128), 128)
        x = xpad[pl.ds(i * 2 + 3, 2), 0:FC].reshape(128, FD).astype(F32)
        stream = x + jnp.dot(attended[tokens, :], w_out[...], preferred_element_type=F32)
        mixed = jnp.dot(rms(stream, gain_f), w_in[...], preferred_element_type=F32)
        gated = (mixed[:, :hidden] * jax.nn.gelu(mixed[:, hidden:])).astype(BF)
        fine = (stream + jnp.dot(gated, w_ffn[...], preferred_element_type=F32)).astype(BF)
        fine_out[tokens, :] = fine
        sorted_rows = jnp.dot(permute, fine, preferred_element_type=F32).astype(BF)
        merged[pl.ds(pl.multiple_of(i * 32, 32), 32), :] = jnp.concatenate(
            [sorted_rows[j * 32 : (j + 1) * 32] for j in range(4)], axis=1
        )
        return carry

    lax.fori_loop(0, FR // 2, feed, 0)

    loads[3].wait()
    coarse = jnp.dot(merged[...], w_merge[...], preferred_element_type=F32).astype(BF)
    coarse_in[...] = coarse
    normed = rms(coarse.astype(F32), gain_coarse[...])
    loads[4].wait()
    low_half = lax.broadcasted_iota(jnp.int32, (CT, 128), 1) < HEAD

    def heads(p, carry):
        def part(which):
            cols = pl.ds(pl.multiple_of(which * CD + p * 256, 256), 256)
            return (
                jnp.dot(normed, w_coarse[:, cols], preferred_element_type=F32)
                .astype(BF)
                .astype(F32)
            )

        query = unit(part(0), blocks)
        key = unit(part(1), blocks)
        value = part(2)
        for j in range(2):
            k2 = key[:, j * 128 : (j + 1) * 128]
            v2 = value[:, j * 128 : (j + 1) * 128]
            even = jnp.where(low_half, k2, pltpu.roll(v2, HEAD, 1))
            odd = jnp.where(low_half, pltpu.roll(k2, HEAD, 1), v2)
            kv_msg[p * 4 + j * 2] = even.astype(BF)
            kv_msg[p * 4 + j * 2 + 1] = odd.astype(BF)
            q2 = query[:, j * 128 : (j + 1) * 128].T.astype(BF)
            q_msg[p * 4 + j * 2] = q2[:HEAD]
            q_msg[p * 4 + j * 2 + 1] = q2[HEAD:]
        return carry

    lax.fori_loop(0, 4, heads, 0)


def coarse_kernel(
    kv_msg,
    q_msg,
    coarse_in,
    scale_coarse,
    w_out_hbm,
    out,
    kv_buf,
    q_buf,
    q_full,
    acc,
    o_buf,
    back,
    w_out,
    load_sem,
    kv_send,
    kv_recv,
    q_send,
    q_recv,
    o_send,
    o_recv,
    g_send,
    g_recv,
):
    row, seq = lax.axis_index("rows"), lax.axis_index("seq")
    x, y, z_lo = row // 8, lax.rem(row // 2, 4), lax.rem(row, 2)
    z_hi, core = seq // 2, lax.rem(seq, 2)
    z = z_hi * 2 + z_lo
    head = y * 4 + z

    def at(dy, dz):
        py, pz = lax.rem(y + dy + 4, 4), lax.rem(z + dz + 4, 4)
        return (x * 8 + py * 2 + lax.rem(pz, 2), (pz // 2) * 2 + core), py * 4 + pz

    sibling = (row, seq + 1 - 2 * core)
    up = (lax.rem(row + 8, 32), seq)
    down = (lax.rem(row + 24, 32), seq)

    load = pltpu.make_async_copy(w_out_hbm, w_out, load_sem)
    load.start()

    offsets = [(dy, dz) for dy in range(4) for dz in range(4)]
    barrier = pltpu.get_barrier_semaphore()
    for dy, dz in offsets[1:]:
        pl.semaphore_signal(barrier, inc=1, device_id=at(dy, dz)[0], device_id_type=MESH)
    for there in (sibling, up, down):
        pl.semaphore_signal(barrier, inc=1, device_id=there, device_id_type=MESH)
    pl.semaphore_wait(barrier, 18)

    def remote(src, dst, send, recv, there):
        copy = pltpu.make_async_remote_copy(
            src_ref=src,
            dst_ref=dst,
            send_sem=send,
            recv_sem=recv,
            device_id=there,
            device_id_type=MESH,
        )
        copy.start()
        return copy

    q_copies, kv_copies = [], []
    for k, (dy, dz) in enumerate(offsets):
        if k == 0:
            continue
        there, their_head = at(dy, dz)
        q_copies.append(
            remote(q_msg.at[their_head], q_buf.at[k], q_send.at[k], q_recv.at[k], there)
        )
        kv_copies.append(
            remote(
                kv_msg.at[their_head],
                kv_buf.at[0, pl.ds(k * CT, CT)],
                kv_send.at[k],
                kv_recv.at[k],
                there,
            )
        )
    kv_buf[0, 0:CT, :] = kv_msg[head]
    q_full[0:HEAD, 0:CT] = q_msg[head]
    q_full[HEAD:, :] = jnp.zeros((HEAD, CHUNK), BF)
    acc[...] = jnp.zeros_like(acc)
    for copy in kv_copies:
        copy.wait()

    half = CHUNK // 2
    first, second = pl.ds(0, half), pl.ds(half, half)
    gathers = {}

    def gather(name, src, dst, there):
        i = len(gathers)
        gathers[name] = remote(src, dst, g_send.at[i], g_recv.at[i], there)

    gather("up", kv_buf.at[0], kv_buf.at[2], up)
    gather("down", kv_buf.at[0], kv_buf.at[4], down)
    gather("own", kv_buf.at[0], kv_buf.at[1], sibling)

    for copy in q_copies:
        copy.wait()
    for k in range(1, 16):
        q_full[0:HEAD, k * CT : (k + 1) * CT] = q_buf[k]

    factor = scale_coarse[0, head] * (LOG2E / HEAD)
    ones = jnp.ones((8, 1024), BF)

    def process(slot):
        def block(i, carry):
            kv = kv_buf[slot, pl.ds(pl.multiple_of(i * 1024, 1024), 1024), :]
            lhs = jnp.concatenate([kv.T[HEAD:], ones], axis=0)
            for u in range(2):
                cols = slice(u * 1024, (u + 1) * 1024)
                scores = jnp.dot(kv, q_full[:, cols], preferred_element_type=F32)
                weights = jnp.exp2(scores * factor).astype(BF)
                acc[:, cols] += jnp.dot(lhs, weights, preferred_element_type=F32)
            return carry

        lax.fori_loop(0, CHUNK // 1024, block, 0)

    process(0)
    gathers["own"].wait_recv()
    process(1)
    gathers["up"].wait_recv()
    gather("up2", kv_buf.at[2, first], kv_buf.at[6, first], up)
    gather("up_sib", kv_buf.at[2], kv_buf.at[3], sibling)
    gathers["down"].wait_recv()
    gather("down2", kv_buf.at[4, second], kv_buf.at[6, second], down)
    gather("down_sib", kv_buf.at[4], kv_buf.at[5], sibling)
    process(2)
    process(4)
    gathers["up_sib"].wait_recv()
    process(3)
    gathers["up2"].wait_recv()
    gathers["down2"].wait_recv()
    gather("two_sib", kv_buf.at[6], kv_buf.at[7], sibling)
    gathers["down_sib"].wait_recv()
    process(5)
    process(6)
    gathers["two_sib"].wait_recv()
    process(7)

    inverse = 1.0 / acc[HEAD : HEAD + 1, :]
    attended = (acc[0:HEAD, :] * inverse).astype(BF)
    o_copies = []
    for k, (dy, dz) in enumerate(offsets):
        part = attended[:, k * CT : (k + 1) * CT]
        if k == 0:
            back[head] = part
            continue
        o_buf[k] = part
        there = at(-dy, -dz)[0]
        o_copies.append(remote(o_buf.at[k], back.at[head], o_send.at[k], o_recv.at[k], there))
    for copy in gathers.values():
        copy.wait_send()
    load.wait()
    for copy in o_copies:
        copy.wait()
    features = back[...].reshape(CD, CT)
    product = lax.dot_general(
        features, w_out[...], (((0,), (0,)), ((), ())), preferred_element_type=F32
    )
    out[...] = (coarse_in[...].astype(F32) + product).astype(BF)


def body(
    image,
    gain_attn,
    w_qkv_fine,
    scale_fine,
    w_out_fine,
    gain_ffn,
    w_ffn_in,
    w_ffn_out,
    w_merge,
    gain_coarse,
    w_qkv_coarse,
    scale_coarse,
    w_out_coarse,
):
    vmem = pl.BlockSpec(memory_space=pltpu.VMEM)
    smem = pl.BlockSpec(memory_space=pltpu.SMEM)
    hbm = pl.BlockSpec(memory_space=pl.ANY)
    dma = pltpu.SemaphoreType.DMA
    fine_out, coarse_in, kv_msg, q_msg = pl.pallas_call(
        fine_kernel,
        out_shape=(
            jax.ShapeDtypeStruct((FR * FC, FD), BF),
            jax.ShapeDtypeStruct((CT, CD), BF),
            jax.ShapeDtypeStruct((NHEAD, CT, 128), BF),
            jax.ShapeDtypeStruct((NHEAD, HEAD, CT), BF),
        ),
        in_specs=[hbm, vmem, vmem, smem, vmem, vmem, hbm, hbm, hbm, vmem, hbm],
        out_specs=(vmem, vmem, vmem, vmem),
        scratch_shapes=[
            pltpu.VMEM((PR, PC, FD), BF),
            pltpu.VMEM((PR * PC, FD), BF),
            pltpu.VMEM((PR * PC, FD + 128), BF),
            pltpu.VMEM((4 * FC, 7 * PC), F32),
            pltpu.VMEM((FR * FC, FD), BF),
            pltpu.VMEM((CT, CD), BF),
            pltpu.VMEM(w_ffn_in.shape, BF),
            pltpu.VMEM(w_ffn_out.shape, BF),
            pltpu.VMEM(w_merge.shape, BF),
            pltpu.VMEM(w_qkv_coarse.shape, BF),
            dma((5,)),
            dma((8,)),
            dma((8,)),
        ],
        compiler_params=pltpu.CompilerParams(
            collective_id=0, has_side_effects=True, vmem_limit_bytes=VMEM_LIMIT
        ),
        name="fine",
    )(
        image,
        gain_attn.reshape(1, -1),
        w_qkv_fine,
        scale_fine.reshape(1, -1),
        w_out_fine,
        gain_ffn.reshape(1, -1),
        w_ffn_in,
        w_ffn_out,
        w_merge,
        gain_coarse.reshape(1, -1),
        w_qkv_coarse,
    )
    coarse_out = pl.pallas_call(
        coarse_kernel,
        out_shape=jax.ShapeDtypeStruct((CT, CD), BF),
        in_specs=[vmem, vmem, vmem, smem, hbm],
        out_specs=vmem,
        scratch_shapes=[
            pltpu.VMEM((8, CHUNK, 128), BF),
            pltpu.VMEM((NHEAD, HEAD, CT), BF),
            pltpu.VMEM((128, CHUNK), BF),
            pltpu.VMEM((HEAD + 8, CHUNK), F32),
            pltpu.VMEM((NHEAD, HEAD, CT), BF),
            pltpu.VMEM((NHEAD, HEAD, CT), BF),
            pltpu.VMEM(w_out_coarse.shape, BF),
            dma,
            dma((16,)),
            dma((16,)),
            dma((16,)),
            dma((16,)),
            dma((16,)),
            dma((16,)),
            dma((8,)),
            dma((8,)),
        ],
        compiler_params=pltpu.CompilerParams(
            collective_id=1, has_side_effects=True, vmem_limit_bytes=VMEM_LIMIT
        ),
        name="coarse",
    )(kv_msg, q_msg, coarse_in, scale_coarse.reshape(1, -1), w_out_coarse)
    return fine_out.reshape(image.shape), coarse_out.reshape(FR // 2, FC // 2, CD)


def solution(mesh):
    placed = (P("rows", "seq", None),) + (P(),) * 12
    return jax.shard_map(
        body,
        mesh=mesh,
        in_specs=placed,
        out_specs=(P("rows", "seq", None), P("rows", "seq", None)),
        check_vma=False,
    )
```

```python
import math

import jax
import jax.numpy as jnp
from jax import lax
from jax.experimental import pallas as pl
from jax.experimental.pallas import tpu as pltpu
from jax.sharding import PartitionSpec as P

HEAD = 64
MESH = pl.DeviceIdType.MESH
BF = jnp.bfloat16
F32 = jnp.float32
LOG2E = math.log2(math.e)

FR, FC, FD = 8, 64, 256
PR, PC = FR + 6, FC + 32
CT, CD = 128, 1024
NHEAD = 16
QUERIES = NHEAD * CT
BLOCK = 1024
NBLOCK = 16
ORDER = (1, 2, 3, 0)
VMEM_LIMIT = 56 * 2**20


def rms(values, gain):
    mean_square = jnp.mean(values * values, axis=-1, keepdims=True)
    return (values * lax.rsqrt(mean_square + 1e-06) * gain).astype(BF)


def dot(a, b):
    return jnp.dot(a, b, preferred_element_type=F32)


def unit(values, blocks):
    square = values * values
    high = square.astype(BF)
    low = (square - high.astype(F32)).astype(BF)
    return values * lax.rsqrt(dot(high, blocks) + dot(low, blocks) + 1e-06)


def kernel(
    image,
    gain_attn,
    w_qkv_hbm,
    scale_fine,
    w_proj_hbm,
    gain_ffn,
    w_in_hbm,
    w_ffn_hbm,
    w_merge_hbm,
    gain_coarse,
    w_coarse_hbm,
    scale_coarse,
    w_out_hbm,
    fine_out,
    out,
    xpad,
    queries,
    keys,
    vals,
    bias,
    attended,
    merged,
    coarse_in,
    kv_msg,
    q_msg,
    kv_buf,
    q_buf,
    q_full,
    acc,
    o_buf,
    back,
    w_qkv,
    w_proj,
    w_in,
    w_ffn,
    w_merge,
    w_coarse,
    w_out,
    load_sem,
    halo_send,
    halo_recv,
    q_send,
    q_recv,
    kv_send,
    kv_recv,
    g_send,
    g_recv,
    o_send,
    o_recv,
):
    row, seq = lax.axis_index("rows"), lax.axis_index("seq")
    n_rows, n_seq = lax.axis_size("rows"), lax.axis_size("seq")
    x, y, z_lo = row // 8, lax.rem(row // 2, 4), lax.rem(row, 2)
    z_hi, core = seq // 2, lax.rem(seq, 2)
    z = z_hi * 2 + z_lo
    head = y * 4 + z

    def at(dy, dz):
        py, pz = lax.rem(y + dy + 4, 4), lax.rem(z + dz + 4, 4)
        return (x * 8 + py * 2 + lax.rem(pz, 2), (pz // 2) * 2 + core)

    def beside(dr, ds):
        return (lax.rem(row + dr + n_rows, n_rows), lax.rem(seq + ds + n_seq, n_seq))

    sibling = (row, seq + 1 - 2 * core)
    up = (lax.rem(row + 8, 32), seq)
    down = (lax.rem(row + 24, 32), seq)
    around = [(dr, ds) for dr in (0, -1, 1) for ds in (0, -1, 1) if (dr, ds) != (0, 0)]
    partners = [(dy, dz) for dy in ORDER for dz in range(4)]
    own = partners.index((0, 0))

    barrier = pltpu.get_barrier_semaphore()
    everyone = [beside(dr, ds) for dr, ds in around]
    everyone += [at(dy, dz) for k, (dy, dz) in enumerate(partners) if k != own]
    everyone += [sibling, up, down]
    for there in everyone:
        pl.semaphore_signal(barrier, inc=1, device_id=there, device_id_type=MESH)

    def load(source, target, i):
        copy = pltpu.make_async_copy(source, target, load_sem.at[i])
        copy.start()
        return copy

    image_load = load(image, xpad.at[pl.ds(3, FR), pl.ds(0, FC)], 0)
    w_qkv_load = load(w_qkv_hbm, w_qkv, 1)
    w_proj_load = load(w_proj_hbm, w_proj, 2)
    w_in_load = load(w_in_hbm, w_in, 3)
    w_ffn_load = load(w_ffn_hbm, w_ffn, 4)
    w_merge_load = load(w_merge_hbm, w_merge, 5)
    w_coarse_load = load(w_coarse_hbm, w_coarse, 6)
    w_out_load = load(w_out_hbm, w_out, 7)

    def remote(src, dst, send, recv, there):
        return pltpu.make_async_remote_copy(
            src_ref=src,
            dst_ref=dst,
            send_sem=send,
            recv_sem=recv,
            device_id=there,
            device_id_type=MESH,
        )

    image_load.wait()
    pl.semaphore_wait(barrier, len(everyone))

    source_rows = {-1: pl.ds(3, 3), 0: pl.ds(3, FR), 1: pl.ds(FR, 3)}
    source_cols = {-1: pl.ds(0, 16), 0: pl.ds(0, FC), 1: pl.ds(FC - 16, 16)}
    target_rows = {-1: pl.ds(FR + 3, 3), 0: pl.ds(3, FR), 1: pl.ds(0, 3)}
    target_cols = {-1: pl.ds(FC + 16, 16), 0: pl.ds(0, FC), 1: pl.ds(FC, 16)}
    halo = [
        remote(
            xpad.at[source_rows[dr], source_cols[ds]],
            xpad.at[target_rows[dr], target_cols[ds]],
            halo_send.at[i],
            halo_recv.at[i],
            beside(dr, ds),
        )
        for i, (dr, ds) in enumerate(around)
    ]
    for copy in halo:
        copy.start()

    group = (lax.broadcasted_iota(jnp.int32, (FD, FD), 0) >> 6) == (
        lax.broadcasted_iota(jnp.int32, (FD, FD), 1) >> 6
    )
    blocks = jnp.where(group, 1.0 / HEAD, 0.0).astype(BF)
    gain = gain_attn[...]
    w_qkv_load.wait()

    def project(tokens, first):
        normed = rms(tokens.astype(F32), gain)
        return dot(normed, w_qkv[:, first:]).astype(BF)

    for i in range(2):
        rows_here = slice(3 + 4 * i, 7 + 4 * i)
        triple = project(xpad[rows_here, 0:FC].reshape(4 * FC, FD), 0)
        queries[i * 4 * FC : (i + 1) * 4 * FC, :] = unit(triple[:, :FD].astype(F32), blocks).astype(
            BF
        )
        unit_keys = unit(triple[:, FD : 2 * FD].astype(F32), blocks).astype(BF)
        keys[rows_here, 0:FC] = unit_keys.reshape(4, FC, FD)
        vals[rows_here, 0:FC] = triple[:, 2 * FD :].reshape(4, FC, FD)

    query_col = lax.broadcasted_iota(jnp.int32, (FC, PC), 0)
    slot = lax.broadcasted_iota(jnp.int32, (FC, PC), 1)
    key_col = jnp.where(slot < FC, slot, jnp.where(slot < FC + 16, slot - FC - 16, slot - 16))
    gap = key_col - query_col
    near = jnp.where((gap >= -3) & (gap <= 3), 0.0, -1e30).astype(F32)
    never = jnp.full((FC, PC), -1e30, F32)
    for r in range(2):
        one = jnp.concatenate([near if r <= j <= r + 6 else never for j in range(8)], axis=1)
        for h in range(4):
            start = (r * 4 + h) * FC
            bias[start : start + FC, :] = one

    for copy in halo:
        copy.wait()

    def halo_keys(pair):
        kv = pair
        return unit(kv[:, :FD].astype(F32), blocks).astype(BF), kv[:, FD:]

    side_keys, side_vals = halo_keys(project(xpad[:, FC:].reshape(PR * 32, FD), FD))
    keys[:, FC:] = side_keys.reshape(PR, 32, FD)
    vals[:, FC:] = side_vals.reshape(PR, 32, FD)
    for rows_here in (slice(0, 3), slice(FR + 3, FR + 6)):
        end_keys, end_vals = halo_keys(project(xpad[rows_here, 0:FC].reshape(3 * FC, FD), FD))
        keys[rows_here, 0:FC] = end_keys.reshape(3, FC, FD)
        vals[rows_here, 0:FC] = end_vals.reshape(3, FC, FD)

    lane_head = lax.broadcasted_iota(jnp.int32, (FC, FD), 1) >> 6
    factor = jnp.concatenate(
        [jnp.full((FC, 1), scale_fine[0, h] * (LOG2E / HEAD), F32) for h in range(4)] * 2, axis=0
    )
    lane = lax.broadcasted_iota(jnp.int32, (1, 8 * PC), 1)
    lane_row = (lane * 683) >> 16
    lane_slot = lane - lane_row * PC
    left_out = (lane_slot >= FC) & (lane_slot < FC + 16) & (seq == 0)
    right_out = (lane_slot >= FC + 16) & (seq == n_seq - 1)
    col_bias = jnp.where(left_out | right_out, -1e30, 0.0).astype(F32)

    def attend(i, carry):
        query = queries[pl.ds(pl.multiple_of(i * 128, 128), 128), :].astype(F32)
        stacked = jnp.concatenate(
            [
                jnp.where(lane_head == h, query[r * FC : (r + 1) * FC], 0.0).astype(BF)
                for r in range(2)
                for h in range(4)
            ],
            axis=0,
        )
        window = pl.ds(i * 2, 8)
        scores = lax.dot_general(
            stacked,
            keys[window].reshape(8 * PC, FD),
            (((1,), (1,)), ((), ())),
            preferred_element_type=F32,
        )
        global_row = row * FR + i * 2 + lane_row - 3
        outside = (global_row < 0) | (global_row >= n_rows * FR)
        key_bias = jnp.where(outside, -1e30, col_bias)
        weights = jnp.exp2(scores * factor + (bias[...] + key_bias))
        total = dot(weights.astype(BF), vals[window].reshape(8 * PC, FD))
        scaled = total * (1.0 / jnp.sum(weights, axis=-1, keepdims=True))
        picked = []
        for r in range(2):
            parts = [scaled[(r * 4 + h) * FC : (r * 4 + h + 1) * FC] for h in range(4)]
            merged_heads = parts[0]
            for h in range(1, 4):
                merged_heads = jnp.where(lane_head == h, parts[h], merged_heads)
            picked.append(merged_heads)
        attended[pl.ds(pl.multiple_of(i * 128, 128), 128), :] = jnp.concatenate(
            picked, axis=0
        ).astype(BF)
        return carry

    lax.fori_loop(0, FR // 2, attend, 0)

    w_proj_load.wait()
    w_in_load.wait()
    w_ffn_load.wait()
    hidden = w_ffn.shape[0]
    take = lax.broadcasted_iota(jnp.int32, (128, 128), 0)
    come = lax.broadcasted_iota(jnp.int32, (128, 128), 1)
    wanted = (take >> 6) * 64 + (take & 31) * 2 + ((take >> 5) & 1)
    permute = jnp.where(come == wanted, 1.0, 0.0).astype(BF)
    gain_f = gain_ffn[...]
    for i in range(2):
        tokens = slice(i * 256, (i + 1) * 256)
        here = xpad[3 + 4 * i : 7 + 4 * i, 0:FC].reshape(256, FD).astype(F32)
        stream = here + dot(attended[tokens, :], w_proj[...])
        normed = rms(stream, gain_f)
        for c in range(0, hidden, 256):
            value = dot(normed, w_in[:, c : c + 256])
            gate = dot(normed, w_in[:, hidden + c : hidden + c + 256])
            gated = (value * jax.nn.gelu(gate)).astype(BF)
            stream = stream + dot(gated, w_ffn[c : c + 256, :])
        fine = stream.astype(BF)
        fine_out[tokens, :] = fine
        for j in range(2):
            part = dot(permute, fine[j * 128 : (j + 1) * 128]).astype(BF)
            start = (i * 2 + j) * 32
            merged[start : start + 32, :] = jnp.concatenate(
                [part[n * 32 : (n + 1) * 32] for n in range(4)], axis=1
            )

    w_merge_load.wait()
    coarse = dot(merged[...], w_merge[...]).astype(BF)
    coarse_in[...] = coarse
    normed = rms(coarse.astype(F32), gain_coarse[...])

    w_coarse_load.wait()

    def heads(which, dy):
        start = which * CD + lax.rem(y + dy, 4) * 256
        cols = pl.ds(pl.multiple_of(start, 256), 256)
        return dot(normed, w_coarse[:, cols]).astype(BF).astype(F32)

    low_half = lax.broadcasted_iota(jnp.int32, (CT, 128), 1) < HEAD
    q_copies, kv_copies = {}, {}
    for n, dy in enumerate(ORDER):
        query = unit(heads(0, dy), blocks)
        for j in range(2):
            turned = query[:, j * 128 : (j + 1) * 128].T.astype(BF)
            q_msg[n * 4 + 2 * j] = turned[:HEAD]
            q_msg[n * 4 + 2 * j + 1] = turned[HEAD:]
        for dz in range(4):
            k = n * 4 + dz
            if k != own:
                source = q_msg.at[n * 4 + lax.rem(z + dz, 4)]
                q_copies[k] = remote(
                    source, q_buf.at[k], q_send.at[k], q_recv.at[k], at(dy, dz)
                )
                q_copies[k].start()
    for n, dy in enumerate(ORDER):
        key = unit(heads(1, dy), blocks)
        value = heads(2, dy)
        for j in range(2):
            k2 = key[:, j * 128 : (j + 1) * 128]
            v2 = value[:, j * 128 : (j + 1) * 128]
            even = jnp.where(low_half, k2, pltpu.roll(v2, HEAD, 1))
            odd = jnp.where(low_half, pltpu.roll(k2, HEAD, 1), v2)
            kv_msg[n * 4 + 2 * j] = even.astype(BF)
            kv_msg[n * 4 + 2 * j + 1] = odd.astype(BF)
        for dz in range(4):
            k = n * 4 + dz
            if k != own:
                source = kv_msg.at[n * 4 + lax.rem(z + dz, 4)]
                target = kv_buf.at[k // 8, pl.ds((k % 8) * CT, CT)]
                kv_copies[k] = remote(source, target, kv_send.at[k], kv_recv.at[k], at(dy, dz))
                kv_copies[k].start()
    own_row = (own % 8) * CT
    kv_buf[own // 8, own_row : own_row + CT, :] = kv_msg[own + z]

    q_full[HEAD:, :] = jnp.zeros((HEAD, QUERIES), BF)
    acc[...] = jnp.zeros_like(acc)
    for k in range(16):
        if k == own:
            part = q_msg[own + z]
        else:
            q_copies[k].wait()
            part = q_buf[k]
        q_full[0:HEAD, k * CT : (k + 1) * CT] = part

    def gather(source, target, there):
        return remote(
            kv_buf.at[source], kv_buf.at[target], g_send.at[target], g_recv.at[target], there
        )

    gathers = {
        2: gather(0, 2, sibling),
        3: gather(1, 3, sibling),
        4: gather(0, 4, up),
        5: gather(0, 5, down),
        6: gather(4, 6, sibling),
        7: gather(5, 7, sibling),
        8: gather(1, 8, up),
        9: gather(1, 9, down),
        10: gather(8, 10, sibling),
        11: gather(9, 11, sibling),
        12: gather(4, 12, up),
        13: gather(9, 13, down),
        14: gather(12, 14, sibling),
        15: gather(13, 15, sibling),
    }
    arrive = {b: ("gather", (b,)) for b in gathers}
    arrive[0] = ("plane", range(0, 8))
    arrive[1] = ("plane", range(8, 16))
    arrive[8] = ("gather", (8, 9))
    arrive[12] = ("gather", (12, 13))
    del arrive[9], arrive[13]
    start_after = {0: (4, 5, 2), 1: (8, 9, 3), 4: (12, 6), 5: (7,), 8: (13, 10, 11), 12: (14, 15)}

    def arrivals(b):
        kind, which = arrive[b]
        for k in which:
            if kind == "gather":
                gathers[k].wait_recv()
            elif k != own:
                kv_copies[k].wait()
        for target in start_after.get(b, ()):
            gathers[target].start()

    head_factor = scale_coarse[0, head] * (LOG2E / HEAD)
    ones = jnp.ones((8, BLOCK), BF)
    half = QUERIES // 2

    def process(b, halves):
        kv = kv_buf[b]
        lhs = jnp.concatenate([kv.T[HEAD:], ones], axis=0)
        for u in halves:
            cols = slice(u * half, (u + 1) * half)
            weights = jnp.exp2(dot(kv, q_full[:, cols]) * head_factor).astype(BF)
            acc[:, cols] += dot(lhs, weights)

    def step(b, carry):
        for block in sorted(arrive):
            if block < 12:
                pl.when(b == block)(lambda block=block: arrivals(block))
        process(b, (0, 1))
        return carry

    lax.fori_loop(0, 12, step, 0)

    o_copies = {}
    for u in range(2):

        def last(b, carry):
            if u == 0:
                for block in (12, 14, 15):
                    pl.when(b == block)(lambda block=block: arrivals(block))
            process(b, (u,))
            return carry

        lax.fori_loop(12, NBLOCK, last, 0)
        cols = slice(u * half, (u + 1) * half)
        inverse = 1.0 / acc[HEAD : HEAD + 1, cols]
        done = (acc[0:HEAD, cols] * inverse).astype(BF)
        for k in range(u * 8, u * 8 + 8):
            dy, dz = partners[k]
            part = done[:, (k % 8) * CT : (k % 8 + 1) * CT]
            if k == own:
                back[head] = part
                continue
            o_buf[k] = part
            o_copies[k] = remote(
                o_buf.at[k], back.at[head], o_send.at[k], o_recv.at[k], at(-dy, -dz)
            )
            o_copies[k].start()

    for b in range(2, NBLOCK):
        gathers[b].wait_send()
    w_out_load.wait()
    total = coarse_in[...].astype(F32)
    for n, dy in enumerate(ORDER):
        for dz in range(4):
            if n * 4 + dz != own:
                o_copies[n * 4 + dz].wait()
        from_y = lax.rem(y + dy, 4)
        features = back[pl.ds(from_y * 4, 4)].reshape(256, CT)
        rows_here = pl.ds(pl.multiple_of(from_y * 256, 256), 256)
        total = total + lax.dot_general(
            features, w_out[rows_here, :], (((0,), (0,)), ((), ())), preferred_element_type=F32
        )
    out[...] = total.astype(BF)


def body(
    image,
    gain_attn,
    w_qkv_fine,
    scale_fine,
    w_out_fine,
    gain_ffn,
    w_ffn_in,
    w_ffn_out,
    w_merge,
    gain_coarse,
    w_qkv_coarse,
    scale_coarse,
    w_out_coarse,
):
    vmem = pl.BlockSpec(memory_space=pltpu.VMEM)
    smem = pl.BlockSpec(memory_space=pltpu.SMEM)
    hbm = pl.BlockSpec(memory_space=pl.ANY)
    dma = pltpu.SemaphoreType.DMA
    weights = (w_qkv_fine, w_out_fine, w_ffn_in, w_ffn_out, w_merge, w_qkv_coarse, w_out_coarse)
    fine_out, coarse_out = pl.pallas_call(
        kernel,
        out_shape=(pltpu.VMEM((FR * FC, FD), BF), pltpu.VMEM((CT, CD), BF)),
        in_specs=[hbm, vmem, hbm, smem, hbm, vmem, hbm, hbm, hbm, vmem, hbm, smem, hbm],
        out_specs=(vmem, vmem),
        scratch_shapes=[
            pltpu.VMEM((PR, PC, FD), BF),
            pltpu.VMEM((FR * FC, FD), BF),
            pltpu.VMEM((PR, PC, FD), BF),
            pltpu.VMEM((PR, PC, FD), BF),
            pltpu.VMEM((8 * FC, 8 * PC), F32),
            pltpu.VMEM((FR * FC, FD), BF),
            pltpu.VMEM((CT, CD), BF),
            pltpu.VMEM((CT, CD), BF),
            pltpu.VMEM((NHEAD, CT, 128), BF),
            pltpu.VMEM((NHEAD, HEAD, CT), BF),
            pltpu.VMEM((NBLOCK, BLOCK, 128), BF),
            pltpu.VMEM((NHEAD, HEAD, CT), BF),
            pltpu.VMEM((128, QUERIES), BF),
            pltpu.VMEM((HEAD + 8, QUERIES), F32),
            pltpu.VMEM((NHEAD, HEAD, CT), BF),
            pltpu.VMEM((NHEAD, HEAD, CT), BF),
        ]
        + [pltpu.VMEM(w.shape, BF) for w in weights]
        + [dma((8,)), dma((8,)), dma((8,))]
        + [dma((16,))] * 8,
        compiler_params=pltpu.CompilerParams(
            collective_id=0, has_side_effects=True, vmem_limit_bytes=VMEM_LIMIT
        ),
        name="window",
    )(
        image,
        gain_attn.reshape(1, -1),
        w_qkv_fine,
        scale_fine.reshape(1, -1),
        w_out_fine,
        gain_ffn.reshape(1, -1),
        w_ffn_in,
        w_ffn_out,
        w_merge,
        gain_coarse.reshape(1, -1),
        w_qkv_coarse,
        scale_coarse.reshape(1, -1),
        w_out_coarse,
    )
    return fine_out.reshape(image.shape), coarse_out.reshape(FR // 2, FC // 2, CD)


def solution(mesh):
    placed = (P("rows", "seq", None),) + (P(),) * 12
    return jax.shard_map(
        body,
        mesh=mesh,
        in_specs=placed,
        out_specs=(P("rows", "seq", None), P("rows", "seq", None)),
        check_vma=False,
    )
```

```python
import math

import jax
import jax.numpy as jnp
from jax import lax
from jax.experimental import pallas as pl
from jax.experimental.pallas import tpu as pltpu
from jax.sharding import PartitionSpec as P

HEAD = 64
MESH = pl.DeviceIdType.MESH
BF = jnp.bfloat16
F32 = jnp.float32
LOG2E = math.log2(math.e)

FR, FC, FD = 8, 64, 256
PR = FR + 6
WINDOW = 8 * FC
SIDE = 128
CT, CD = 128, 1024
NHEAD = 16
HT = CT // 2
QUERIES = NHEAD * CT
BLOCK = 1024
NBLOCK = 16
ORDER = (1, 2, 3, 0)
VMEM_LIMIT = 56 * 2**20


def rms(values, gain):
    mean_square = jnp.mean(values * values, axis=-1, keepdims=True)
    return (values * lax.rsqrt(mean_square + 1e-06) * gain).astype(BF)


def dot(a, b):
    return jnp.dot(a, b, preferred_element_type=F32)


def unit(values, blocks):
    square = values * values
    high = square.astype(BF)
    low = (square - high.astype(F32)).astype(BF)
    return values * lax.rsqrt(dot(high, blocks) + dot(low, blocks) + 1e-06)


def kernel(
    image,
    gain_attn,
    w_qkv_hbm,
    scale_fine,
    w_proj_hbm,
    gain_ffn,
    w_in_hbm,
    w_ffn_hbm,
    w_merge_hbm,
    gain_coarse,
    w_coarse_hbm,
    scale_coarse,
    w_out_hbm,
    fine_out,
    out,
    xpad,
    packed,
    side,
    queries,
    keys,
    vals,
    side_keys,
    side_vals,
    bias,
    side_gap,
    attended,
    merged,
    coarse_in,
    messages,
    landed,
    kv_buf,
    q_buf,
    q_full,
    acc,
    o_buf,
    back,
    w_qkv,
    w_proj,
    w_in,
    w_ffn,
    w_merge,
    w_coarse,
    w_out,
    load_sem,
    halo_send,
    halo_recv,
    x_send,
    x_recv,
    g_send,
    g_recv,
    o_send,
    o_recv,
):
    row, seq = lax.axis_index("rows"), lax.axis_index("seq")
    n_rows, n_seq = lax.axis_size("rows"), lax.axis_size("seq")
    x, y, z_lo = row // 8, lax.rem(row // 2, 4), lax.rem(row, 2)
    z_hi, core = seq // 2, lax.rem(seq, 2)
    z = z_hi * 2 + z_lo
    head = y * 4 + z

    def at(dy, dz):
        py, pz = lax.rem(y + dy + 4, 4), lax.rem(z + dz + 4, 4)
        return (x * 8 + py * 2 + lax.rem(pz, 2), (pz // 2) * 2 + core)

    def beside(dr, ds):
        return (lax.rem(row + dr + n_rows, n_rows), lax.rem(seq + ds + n_seq, n_seq))

    sibling = (row, seq + 1 - 2 * core)
    up = (lax.rem(row + 8, 32), seq)
    down = (lax.rem(row + 24, 32), seq)
    around = [(dr, ds) for dr in (0, -1, 1) for ds in (0, -1, 1) if (dr, ds) != (0, 0)]
    partners = [(dy, dz) for dy in ORDER for dz in range(4)]
    own = partners.index((0, 0))

    barrier = pltpu.get_barrier_semaphore()
    everyone = [beside(dr, ds) for dr, ds in around]
    everyone += [at(dy, dz) for k, (dy, dz) in enumerate(partners) if k != own]
    everyone += [sibling, up, down]
    for there in everyone:
        pl.semaphore_signal(barrier, inc=1, device_id=there, device_id_type=MESH)

    def load(source, target, i):
        copy = pltpu.make_async_copy(source, target, load_sem.at[i])
        copy.start()
        return copy

    image_load = load(image, xpad.at[pl.ds(3, FR)], 0)
    w_qkv_load = load(w_qkv_hbm, w_qkv, 1)
    w_proj_load = load(w_proj_hbm, w_proj, 2)
    w_in_load = load(w_in_hbm, w_in, 3)
    w_ffn_load = load(w_ffn_hbm, w_ffn, 4)
    w_merge_load = load(w_merge_hbm, w_merge, 5)
    w_coarse_load = load(w_coarse_hbm, w_coarse, 6)
    w_out_load = load(w_out_hbm, w_out, 7)

    def remote(src, dst, send, recv, there):
        return pltpu.make_async_remote_copy(
            src_ref=src,
            dst_ref=dst,
            send_sem=send,
            recv_sem=recv,
            device_id=there,
            device_id_type=MESH,
        )

    image_load.wait()
    pl.semaphore_wait(barrier, len(everyone))

    halo = {}

    def send_halo(place, source, target):
        i = len(halo)
        halo[place] = remote(source, target, halo_send.at[i], halo_recv.at[i], beside(*place))
        halo[place].start()

    send_halo((-1, 0), xpad.at[pl.ds(3, 3)], xpad.at[pl.ds(FR + 3, 3)])
    send_halo((1, 0), xpad.at[pl.ds(FR, 3)], xpad.at[pl.ds(0, 3)])
    take = lax.broadcasted_iota(jnp.int32, (64, FR * FC), 0)
    come = lax.broadcasted_iota(jnp.int32, (64, FR * FC), 1)
    wanted = ((take & 31) >> 2) * FC + (take & 3) + (take >> 5) * (FC - 4)
    pick = jnp.where(come == wanted, 1.0, 0.0).astype(BF)
    packed[...] = dot(pick, xpad[3 : 3 + FR].reshape(FR * FC, FD)).astype(BF)
    for ds, start in ((-1, 0), (1, 32)):
        there = 1 if ds == -1 else 0
        send_halo((0, ds), packed.at[pl.ds(start, 32)], side.at[there, pl.ds(16, 32)])
        send_halo((-1, ds), packed.at[pl.ds(start, 16)], side.at[there, pl.ds(48, 16)])
        send_halo((1, ds), packed.at[pl.ds(start + 16, 16)], side.at[there, pl.ds(0, 16)])

    group = (lax.broadcasted_iota(jnp.int32, (FD, FD), 0) >> 6) == (
        lax.broadcasted_iota(jnp.int32, (FD, FD), 1) >> 6
    )
    blocks = jnp.where(group, 1.0 / HEAD, 0.0).astype(BF)
    gain = gain_attn[...]
    w_qkv_load.wait()

    def project(tokens, first):
        normed = rms(tokens.astype(F32), gain)
        return dot(normed, w_qkv[:, first:]).astype(BF)

    def unit_bf(values):
        return unit(values.astype(F32), blocks).astype(BF)

    for i in range(2):
        rows_here = slice(3 + 4 * i, 7 + 4 * i)
        triple = project(xpad[rows_here].reshape(4 * FC, FD), 0)
        queries[i * 4 * FC : (i + 1) * 4 * FC, :] = unit_bf(triple[:, :FD])
        keys[rows_here] = unit_bf(triple[:, FD : 2 * FD]).reshape(4, FC, FD)
        vals[rows_here] = triple[:, 2 * FD :].reshape(4, FC, FD)

    gap = lax.broadcasted_iota(jnp.int32, (FC, FC), 1) - lax.broadcasted_iota(
        jnp.int32, (FC, FC), 0
    )
    near = jnp.where((gap >= -3) & (gap <= 3), 0.0, -1e30).astype(F32)
    never = jnp.full((FC, FC), -1e30, F32)
    query_col = lax.broadcasted_iota(jnp.int32, (FC, SIDE), 0)
    slot = lax.broadcasted_iota(jnp.int32, (FC, SIDE), 1)
    right = slot >> 6
    side_row = ((slot & 63) >> 2) - 1
    side_col = (slot & 3) - 4 + right * (FC + 4)
    side_global = row * FR + side_row - 3
    side_near = (side_col - query_col >= -3) & (side_col - query_col <= 3)
    side_near = side_near & (side_global >= 0) & (side_global < n_rows * FR)
    side_near = side_near & ((right > 0) | (seq > 0)) & ((right < 1) | (seq < n_seq - 1))
    for r in range(2):
        one = jnp.concatenate([near if r <= j <= r + 6 else never for j in range(8)], axis=1)
        gap_row = jnp.where(side_near, side_row - r, 1000)
        for h in range(4):
            start = (r * 4 + h) * FC
            bias[start : start + FC, :] = one
            side_gap[start : start + FC, :] = gap_row

    lane_head = lax.broadcasted_iota(jnp.int32, (FC, FD), 1) >> 6
    factor = jnp.concatenate(
        [jnp.full((FC, 1), scale_fine[0, h] * (LOG2E / HEAD), F32) for h in range(4)] * 2, axis=0
    )
    window_row = lax.broadcasted_iota(jnp.int32, (1, WINDOW), 1) >> 6
    last_dims = (((1,), (1,)), ((), ()))

    def attend(i):
        query = queries[i * 128 : (i + 1) * 128, :].astype(F32)
        stacked = jnp.concatenate(
            [
                jnp.where(lane_head == h, query[r * FC : (r + 1) * FC], 0.0).astype(BF)
                for r in range(2)
                for h in range(4)
            ],
            axis=0,
        )
        window = slice(i * 2, i * 2 + 8)
        scores = lax.dot_general(
            stacked, keys[window].reshape(WINDOW, FD), last_dims, preferred_element_type=F32
        )
        side_scores = lax.dot_general(
            stacked, side_keys[...], last_dims, preferred_element_type=F32
        )
        global_row = row * FR + i * 2 + window_row - 3
        outside = (global_row < 0) | (global_row >= n_rows * FR)
        key_bias = jnp.where(outside, -1e30, 0.0).astype(F32)
        weights = jnp.exp2(scores * factor + (bias[...] + key_bias))
        off = side_gap[...] - i * 2
        side_weights = jnp.where(
            (off >= 0) & (off <= 6), jnp.exp2(side_scores * factor), 0.0
        )
        total = dot(weights.astype(BF), vals[window].reshape(WINDOW, FD)) + dot(
            side_weights.astype(BF), side_vals[...]
        )
        weight_sum = side_weights
        for j in range(0, WINDOW, 128):
            weight_sum = weight_sum + weights[:, j : j + 128]
        scaled = total * (1.0 / jnp.sum(weight_sum, axis=-1, keepdims=True))
        picked = []
        for r in range(2):
            parts = [scaled[(r * 4 + h) * FC : (r * 4 + h + 1) * FC] for h in range(4)]
            merged_heads = parts[0]
            for h in range(1, 4):
                merged_heads = jnp.where(lane_head == h, parts[h], merged_heads)
            picked.append(merged_heads)
        attended[i * 128 : (i + 1) * 128, :] = jnp.concatenate(picked, axis=0).astype(BF)

    def end_rows(rows_here):
        kv = project(xpad[rows_here].reshape(3 * FC, FD), FD)
        keys[rows_here] = unit_bf(kv[:, :FD]).reshape(3, FC, FD)
        vals[rows_here] = kv[:, FD:].reshape(3, FC, FD)

    hidden = w_ffn.shape[0]
    take = lax.broadcasted_iota(jnp.int32, (128, 128), 0)
    come = lax.broadcasted_iota(jnp.int32, (128, 128), 1)
    wanted = (take >> 6) * 64 + (take & 31) * 2 + ((take >> 5) & 1)
    permute = jnp.where(come == wanted, 1.0, 0.0).astype(BF)
    gain_f = gain_ffn[...]

    def feed(i):
        tokens = slice(i * 256, (i + 1) * 256)
        here = xpad[3 + 4 * i : 7 + 4 * i].reshape(256, FD).astype(F32)
        stream = here + dot(attended[tokens, :], w_proj[...])
        normed = rms(stream, gain_f)
        for c in range(0, hidden, 256):
            value = dot(normed, w_in[:, c : c + 256])
            gate = dot(normed, w_in[:, hidden + c : hidden + c + 256])
            gated = (value * jax.nn.gelu(gate)).astype(BF)
            stream = stream + dot(gated, w_ffn[c : c + 256, :])
        fine = stream.astype(BF)
        fine_out[tokens, :] = fine
        for j in range(2):
            part = dot(permute, fine[j * 128 : (j + 1) * 128]).astype(BF)
            start = (i * 2 + j) * 32
            merged[start : start + 32, :] = jnp.concatenate(
                [part[n * 32 : (n + 1) * 32] for n in range(4)], axis=1
            )

    low_half = lax.broadcasted_iota(jnp.int32, (HT, 128), 1) < HEAD
    copies = {}

    def exchange(t):
        tokens = slice(t * HT, (t + 1) * HT)
        coarse = dot(merged[tokens, :], w_merge[...]).astype(BF)
        coarse_in[tokens, :] = coarse
        normed = rms(coarse.astype(F32), gain_coarse[...])

        def heads(which, dy):
            start = which * CD + lax.rem(y + dy, 4) * 256
            cols = pl.ds(pl.multiple_of(start, 256), 256)
            return dot(normed, w_coarse[:, cols]).astype(BF).astype(F32)

        def query_part(n, dy):
            query = unit(heads(0, dy), blocks)
            for j in range(2):
                pair = query[:, j * 128 : (j + 1) * 128]
                turned = jnp.concatenate([pair, pair], axis=0).T
                for e in range(2):
                    first, second = turned[e * 64 : e * 64 + 32], turned[e * 64 + 32 : e * 64 + 64]
                    part = jnp.where(low_half[:32], first, second).astype(BF)
                    messages[t, n * 4 + 2 * j + e, HT:] = part

        def key_part(n, dy):
            key = unit(heads(1, dy), blocks)
            value = heads(2, dy)
            for j in range(2):
                k2 = key[:, j * 128 : (j + 1) * 128]
                v2 = value[:, j * 128 : (j + 1) * 128]
                even = jnp.where(low_half, k2, pltpu.roll(v2, HEAD, 1))
                odd = jnp.where(low_half, pltpu.roll(k2, HEAD, 1), v2)
                messages[t, n * 4 + 2 * j, :HT] = even.astype(BF)
                messages[t, n * 4 + 2 * j + 1, :HT] = odd.astype(BF)

        def send(n, dy, name, rows_here, target):
            for dz in range(4):
                k = n * 4 + dz
                if k != own:
                    copies[name, k] = remote(
                        messages.at[t, n * 4 + lax.rem(z + dz, 4), rows_here],
                        target(k),
                        x_send.at[name, k],
                        x_recv.at[name, k],
                        at(dy, dz),
                    )
                    copies[name, k].start()

        if t == 0:
            for n, dy in enumerate(ORDER):
                query_part(n, dy)
                key_part(n, dy)
                send(n, dy, 0, pl.ds(0, 96), lambda k: landed.at[k])
        else:
            for n, dy in enumerate(ORDER):
                query_part(n, dy)
                send(n, dy, 1, pl.ds(HT, 32), lambda k: q_buf.at[k])
            for n, dy in enumerate(ORDER):
                key_part(n, dy)
                send(n, dy, 2, pl.ds(0, HT), lambda k: kv_buf.at[2, pl.ds(k * HT, HT)])
            kv_buf[2, own * HT : (own + 1) * HT, :] = messages[1, own + z, :HT]

    for place in halo:
        if place != (1, 0) and place != (-1, 0):
            halo[place].wait()
    side_kv = project(side[...].reshape(SIDE, FD), FD)
    side_keys[...] = unit_bf(side_kv[:, :FD])
    side_vals[...] = side_kv[:, FD:]
    halo[1, 0].wait()
    end_rows(slice(0, 3))
    attend(0)
    attend(1)
    w_proj_load.wait()
    w_in_load.wait()
    w_ffn_load.wait()
    feed(0)
    w_merge_load.wait()
    w_coarse_load.wait()
    exchange(0)
    halo[-1, 0].wait()
    end_rows(slice(FR + 3, FR + 6))
    attend(2)
    attend(3)
    feed(1)
    exchange(1)

    q_full[HEAD:, :] = jnp.zeros((HEAD, QUERIES), BF)
    acc[...] = jnp.zeros_like(acc)
    def gather(source, target, there):
        return remote(
            kv_buf.at[source], kv_buf.at[target], g_send.at[target], g_recv.at[target], there
        )

    gathers = {
        1: gather(0, 1, sibling),
        3: gather(2, 3, sibling),
        4: gather(0, 4, up),
        5: gather(0, 5, down),
        6: gather(4, 6, sibling),
        7: gather(5, 7, sibling),
        8: gather(2, 8, up),
        9: gather(2, 9, down),
        10: gather(8, 10, sibling),
        11: gather(9, 11, sibling),
        12: gather(4, 12, up),
        13: gather(9, 13, down),
        14: gather(12, 14, sibling),
        15: gather(13, 15, sibling),
    }
    arrive = {b: ("gather", (b,)) for b in gathers}
    arrive[0] = ("plane", [(0, k) for k in range(16)])
    arrive[2] = ("plane", [(2, k) for k in range(16)])
    arrive[8] = ("gather", (8, 9))
    arrive[12] = ("gather", (12, 13))
    del arrive[9], arrive[13]
    start_after = {0: (4, 5, 1), 2: (8, 9, 3), 4: (12, 6), 5: (7,), 8: (13, 10, 11), 12: (14, 15)}

    def arrivals(b):
        kind, which = arrive[b]
        for k in which:
            if kind == "gather":
                gathers[k].wait_recv()
            elif k[1] != own:
                copies[k].wait()
        if b == 0:
            for k in range(16):
                part = messages[0, own + z, :HT] if k == own else landed[k, :HT]
                kv_buf[0, k * HT : (k + 1) * HT, :] = part
        for target in start_after.get(b, ()):
            gathers[target].start()

    arrivals(0)
    for k in range(16):
        if k == own:
            parts = [messages[t, own + z, HT:] for t in range(2)]
        else:
            copies[1, k].wait()
            parts = [landed[k, HT:], q_buf[k]]
        parts = [part.astype(F32) for part in parts]
        top = jnp.where(low_half[:32], parts[0], pltpu.roll(parts[1], HEAD, 1))
        end = jnp.where(low_half[:32], pltpu.roll(parts[0], HEAD, 1), parts[1])
        q_full[0:HEAD, k * CT : (k + 1) * CT] = jnp.concatenate([top, end], axis=0).astype(BF)

    head_factor = scale_coarse[0, head] * (LOG2E / HEAD)
    ones = jnp.ones((8, BLOCK), BF)
    half = QUERIES // 2

    def process(b, halves):
        kv = kv_buf[b]
        lhs = jnp.concatenate([kv.T[HEAD:], ones], axis=0)
        for u in halves:
            cols = slice(u * half, (u + 1) * half)
            weights = jnp.exp2(dot(kv, q_full[:, cols]) * head_factor).astype(BF)
            acc[:, cols] += dot(lhs, weights)

    def step(b, carry):
        for block in sorted(arrive):
            if 0 < block < 12:
                pl.when(b == block)(lambda block=block: arrivals(block))
        process(b, (0, 1))
        return carry

    lax.fori_loop(0, 12, step, 0)

    o_copies = {}
    for u in range(2):

        def last(b, carry):
            if u == 0:
                for block in (12, 14, 15):
                    pl.when(b == block)(lambda block=block: arrivals(block))
            process(b, (u,))
            return carry

        lax.fori_loop(12, NBLOCK, last, 0)
        cols = slice(u * half, (u + 1) * half)
        inverse = 1.0 / acc[HEAD : HEAD + 1, cols]
        done = (acc[0:HEAD, cols] * inverse).astype(BF)
        for k in range(u * 8, u * 8 + 8):
            dy, dz = partners[k]
            part = done[:, (k % 8) * CT : (k % 8 + 1) * CT]
            if k == own:
                back[head] = part
                continue
            o_buf[k] = part
            o_copies[k] = remote(
                o_buf.at[k], back.at[head], o_send.at[k], o_recv.at[k], at(-dy, -dz)
            )
            o_copies[k].start()

    for copy in gathers.values():
        copy.wait_send()
    w_out_load.wait()
    total = coarse_in[...].astype(F32)
    for n, dy in enumerate(ORDER):
        for dz in range(4):
            if n * 4 + dz != own:
                o_copies[n * 4 + dz].wait()
        from_y = lax.rem(y + dy, 4)
        features = back[pl.ds(from_y * 4, 4)].reshape(256, CT)
        rows_here = pl.ds(pl.multiple_of(from_y * 256, 256), 256)
        total = total + lax.dot_general(
            features, w_out[rows_here, :], (((0,), (0,)), ((), ())), preferred_element_type=F32
        )
    out[...] = total.astype(BF)


def body(
    image,
    gain_attn,
    w_qkv_fine,
    scale_fine,
    w_out_fine,
    gain_ffn,
    w_ffn_in,
    w_ffn_out,
    w_merge,
    gain_coarse,
    w_qkv_coarse,
    scale_coarse,
    w_out_coarse,
):
    vmem = pl.BlockSpec(memory_space=pltpu.VMEM)
    smem = pl.BlockSpec(memory_space=pltpu.SMEM)
    hbm = pl.BlockSpec(memory_space=pl.ANY)
    dma = pltpu.SemaphoreType.DMA
    weights = (w_qkv_fine, w_out_fine, w_ffn_in, w_ffn_out, w_merge, w_qkv_coarse, w_out_coarse)
    fine_out, coarse_out = pl.pallas_call(
        kernel,
        out_shape=(pltpu.VMEM((FR * FC, FD), BF), pltpu.VMEM((CT, CD), BF)),
        in_specs=[hbm, vmem, hbm, smem, hbm, vmem, hbm, hbm, hbm, vmem, hbm, smem, hbm],
        out_specs=(vmem, vmem),
        scratch_shapes=[
            pltpu.VMEM((PR, FC, FD), BF),
            pltpu.VMEM((64, FD), BF),
            pltpu.VMEM((2, 64, FD), BF),
            pltpu.VMEM((FR * FC, FD), BF),
            pltpu.VMEM((PR, FC, FD), BF),
            pltpu.VMEM((PR, FC, FD), BF),
            pltpu.VMEM((SIDE, FD), BF),
            pltpu.VMEM((SIDE, FD), BF),
            pltpu.VMEM((8 * FC, WINDOW), F32),
            pltpu.VMEM((8 * FC, SIDE), jnp.int32),
            pltpu.VMEM((FR * FC, FD), BF),
            pltpu.VMEM((CT, CD), BF),
            pltpu.VMEM((CT, CD), BF),
            pltpu.VMEM((2, NHEAD, HT + HEAD // 2, 128), BF),
            pltpu.VMEM((NHEAD, HT + HEAD // 2, 128), BF),
            pltpu.VMEM((NBLOCK, BLOCK, 128), BF),
            pltpu.VMEM((NHEAD, HEAD // 2, 128), BF),
            pltpu.VMEM((128, QUERIES), BF),
            pltpu.VMEM((HEAD + 8, QUERIES), F32),
            pltpu.VMEM((NHEAD, HEAD, CT), BF),
            pltpu.VMEM((NHEAD, HEAD, CT), BF),
        ]
        + [pltpu.VMEM(w.shape, BF) for w in weights]
        + [dma((8,)), dma((8,)), dma((8,))]
        + [dma((3, 16))] * 2
        + [dma((16,))] * 4,
        compiler_params=pltpu.CompilerParams(
            collective_id=0, has_side_effects=True, vmem_limit_bytes=VMEM_LIMIT
        ),
        name="window",
    )(
        image,
        gain_attn.reshape(1, -1),
        w_qkv_fine,
        scale_fine.reshape(1, -1),
        w_out_fine,
        gain_ffn.reshape(1, -1),
        w_ffn_in,
        w_ffn_out,
        w_merge,
        gain_coarse.reshape(1, -1),
        w_qkv_coarse,
        scale_coarse.reshape(1, -1),
        w_out_coarse,
    )
    return fine_out.reshape(image.shape), coarse_out.reshape(FR // 2, FC // 2, CD)


def solution(mesh):
    placed = (P("rows", "seq", None),) + (P(),) * 12
    return jax.shard_map(
        body,
        mesh=mesh,
        in_specs=placed,
        out_specs=(P("rows", "seq", None), P("rows", "seq", None)),
        check_vma=False,
    )
```

```python
import math

import jax
import jax.numpy as jnp
from jax import lax
from jax.experimental import pallas as pl
from jax.experimental.pallas import tpu as pltpu
from jax.sharding import PartitionSpec as P

HEAD = 64
MESH = pl.DeviceIdType.MESH
BF = jnp.bfloat16
F32 = jnp.float32
LOG2E = math.log2(math.e)

FR, FC, FD = 8, 64, 256
PR = FR + 6
WINDOW = 8 * FC
SIDE = 128
CT, CD = 128, 1024
NHEAD = 16
HT = CT // 2
QUERIES = NHEAD * CT
BLOCK = 1024
NBLOCK = 16
ORDER = (1, 2, 3, 0)
VMEM_LIMIT = 56 * 2**20


def rms(values, gain):
    mean_square = jnp.mean(values * values, axis=-1, keepdims=True)
    return (values * lax.rsqrt(mean_square + 1e-06) * gain).astype(BF)


def dot(a, b):
    return jnp.dot(a, b, preferred_element_type=F32)


def unit(values, blocks):
    square = values * values
    high = square.astype(BF)
    low = (square - high.astype(F32)).astype(BF)
    return values * lax.rsqrt(dot(high, blocks) + dot(low, blocks) + 1e-06)


def kernel(
    image,
    gain_attn,
    w_qkv_hbm,
    scale_fine,
    w_proj_hbm,
    gain_ffn,
    w_in_hbm,
    w_ffn_hbm,
    w_merge_hbm,
    gain_coarse,
    w_coarse_hbm,
    scale_coarse,
    w_out_hbm,
    fine_out,
    out,
    xpad,
    packed,
    side,
    queries,
    keys,
    vals,
    side_keys,
    side_vals,
    bias,
    side_gap,
    attended,
    merged,
    coarse_in,
    messages,
    landed,
    kv_buf,
    q_buf,
    q_full,
    acc,
    o_buf,
    back,
    w_qkv,
    w_proj,
    w_in,
    w_ffn,
    w_merge,
    w_coarse,
    w_out,
    load_sem,
    halo_send,
    halo_recv,
    x_send,
    x_recv,
    g_send,
    g_recv,
    o_send,
    o_recv,
):
    row, seq = lax.axis_index("rows"), lax.axis_index("seq")
    n_rows, n_seq = lax.axis_size("rows"), lax.axis_size("seq")
    x, y, z_lo = row // 8, lax.rem(row // 2, 4), lax.rem(row, 2)
    z_hi, core = seq // 2, lax.rem(seq, 2)
    z = z_hi * 2 + z_lo
    head = y * 4 + z

    def at(dy, dz):
        py, pz = lax.rem(y + dy + 4, 4), lax.rem(z + dz + 4, 4)
        return (x * 8 + py * 2 + lax.rem(pz, 2), (pz // 2) * 2 + core)

    def beside(dr, ds):
        return (lax.rem(row + dr + n_rows, n_rows), lax.rem(seq + ds + n_seq, n_seq))

    sibling = (row, seq + 1 - 2 * core)
    up = (lax.rem(row + 8, 32), seq)
    down = (lax.rem(row + 24, 32), seq)
    around = [(dr, ds) for dr in (0, -1, 1) for ds in (0, -1, 1) if (dr, ds) != (0, 0)]
    partners = [(dy, dz) for dy in ORDER for dz in range(4)]
    own = partners.index((0, 0))

    barrier = pltpu.get_barrier_semaphore()
    everyone = [beside(dr, ds) for dr, ds in around]
    everyone += [at(dy, dz) for k, (dy, dz) in enumerate(partners) if k != own]
    everyone += [sibling, up, down]
    for there in everyone:
        pl.semaphore_signal(barrier, inc=1, device_id=there, device_id_type=MESH)

    def load(source, target, i):
        copy = pltpu.make_async_copy(source, target, load_sem.at[i])
        copy.start()
        return copy

    image_load = load(image, xpad.at[pl.ds(3, FR)], 0)
    w_qkv_load = load(w_qkv_hbm, w_qkv, 1)
    w_proj_load = load(w_proj_hbm, w_proj, 2)
    w_in_load = load(w_in_hbm, w_in, 3)
    w_ffn_load = load(w_ffn_hbm, w_ffn, 4)
    w_merge_load = load(w_merge_hbm, w_merge, 5)
    w_coarse_load = load(w_coarse_hbm, w_coarse, 6)
    w_out_load = load(w_out_hbm, w_out, 7)

    def remote(src, dst, send, recv, there):
        return pltpu.make_async_remote_copy(
            src_ref=src,
            dst_ref=dst,
            send_sem=send,
            recv_sem=recv,
            device_id=there,
            device_id_type=MESH,
        )

    image_load.wait()
    pl.semaphore_wait(barrier, len(everyone))

    halo = {}

    def send_halo(place, source, target):
        i = len(halo)
        halo[place] = remote(source, target, halo_send.at[i], halo_recv.at[i], beside(*place))
        halo[place].start()

    send_halo((-1, 0), xpad.at[pl.ds(3, 3)], xpad.at[pl.ds(FR + 3, 3)])
    send_halo((1, 0), xpad.at[pl.ds(FR, 3)], xpad.at[pl.ds(0, 3)])
    take = lax.broadcasted_iota(jnp.int32, (64, FR * FC), 0)
    come = lax.broadcasted_iota(jnp.int32, (64, FR * FC), 1)
    wanted = ((take & 31) >> 2) * FC + (take & 3) + (take >> 5) * (FC - 4)
    pick = jnp.where(come == wanted, 1.0, 0.0).astype(BF)
    packed[...] = dot(pick, xpad[3 : 3 + FR].reshape(FR * FC, FD)).astype(BF)
    for ds, start in ((-1, 0), (1, 32)):
        there = 1 if ds == -1 else 0
        send_halo((0, ds), packed.at[pl.ds(start, 32)], side.at[there, pl.ds(16, 32)])
        send_halo((-1, ds), packed.at[pl.ds(start, 16)], side.at[there, pl.ds(48, 16)])
        send_halo((1, ds), packed.at[pl.ds(start + 16, 16)], side.at[there, pl.ds(0, 16)])

    group = (lax.broadcasted_iota(jnp.int32, (FD, FD), 0) >> 6) == (
        lax.broadcasted_iota(jnp.int32, (FD, FD), 1) >> 6
    )
    blocks = jnp.where(group, 1.0 / HEAD, 0.0).astype(BF)
    gain = gain_attn[...]
    w_qkv_load.wait()

    def project(tokens, first):
        normed = rms(tokens.astype(F32), gain)
        return dot(normed, w_qkv[:, first:]).astype(BF)

    def unit_bf(values):
        return unit(values.astype(F32), blocks).astype(BF)

    for i in range(2):
        rows_here = slice(3 + 4 * i, 7 + 4 * i)
        triple = project(xpad[rows_here].reshape(4 * FC, FD), 0)
        queries[i * 4 * FC : (i + 1) * 4 * FC, :] = unit_bf(triple[:, :FD])
        keys[rows_here] = unit_bf(triple[:, FD : 2 * FD]).reshape(4, FC, FD)
        vals[rows_here] = triple[:, 2 * FD :].reshape(4, FC, FD)

    gap = lax.broadcasted_iota(jnp.int32, (FC, FC), 1) - lax.broadcasted_iota(
        jnp.int32, (FC, FC), 0
    )
    near = jnp.where((gap >= -3) & (gap <= 3), 0.0, -1e30).astype(F32)
    never = jnp.full((FC, FC), -1e30, F32)
    query_col = lax.broadcasted_iota(jnp.int32, (FC, SIDE), 0)
    slot = lax.broadcasted_iota(jnp.int32, (FC, SIDE), 1)
    right = slot >> 6
    side_row = ((slot & 63) >> 2) - 1
    side_col = (slot & 3) - 4 + right * (FC + 4)
    side_global = row * FR + side_row - 3
    side_near = (side_col - query_col >= -3) & (side_col - query_col <= 3)
    side_near = side_near & (side_global >= 0) & (side_global < n_rows * FR)
    side_near = side_near & ((right > 0) | (seq > 0)) & ((right < 1) | (seq < n_seq - 1))
    for r in range(2):
        one = jnp.concatenate([near if r <= j <= r + 6 else never for j in range(8)], axis=1)
        gap_row = jnp.where(side_near, side_row - r, 1000)
        for h in range(4):
            start = (r * 4 + h) * FC
            bias[start : start + FC, :] = one
            side_gap[start : start + FC, :] = gap_row

    lane_head = lax.broadcasted_iota(jnp.int32, (FC, FD), 1) >> 6
    factor = jnp.concatenate(
        [jnp.full((FC, 1), scale_fine[0, h] * (LOG2E / HEAD), F32) for h in range(4)] * 2, axis=0
    )
    window_row = lax.broadcasted_iota(jnp.int32, (1, WINDOW), 1) >> 6
    last_dims = (((1,), (1,)), ((), ()))

    def attend(i):
        query = queries[i * 128 : (i + 1) * 128, :].astype(F32)
        stacked = jnp.concatenate(
            [
                jnp.where(lane_head == h, query[r * FC : (r + 1) * FC], 0.0).astype(BF)
                for r in range(2)
                for h in range(4)
            ],
            axis=0,
        )
        window = slice(i * 2, i * 2 + 8)
        scores = lax.dot_general(
            stacked, keys[window].reshape(WINDOW, FD), last_dims, preferred_element_type=F32
        )
        side_scores = lax.dot_general(
            stacked, side_keys[...], last_dims, preferred_element_type=F32
        )
        global_row = row * FR + i * 2 + window_row - 3
        outside = (global_row < 0) | (global_row >= n_rows * FR)
        key_bias = jnp.where(outside, -1e30, 0.0).astype(F32)
        weights = jnp.exp2(scores * factor + (bias[...] + key_bias))
        off = side_gap[...] - i * 2
        side_weights = jnp.where(
            (off >= 0) & (off <= 6), jnp.exp2(side_scores * factor), 0.0
        )
        total = dot(weights.astype(BF), vals[window].reshape(WINDOW, FD)) + dot(
            side_weights.astype(BF), side_vals[...]
        )
        weight_sum = side_weights
        for j in range(0, WINDOW, 128):
            weight_sum = weight_sum + weights[:, j : j + 128]
        scaled = total * (1.0 / jnp.sum(weight_sum, axis=-1, keepdims=True))
        picked = []
        for r in range(2):
            parts = [scaled[(r * 4 + h) * FC : (r * 4 + h + 1) * FC] for h in range(4)]
            merged_heads = parts[0]
            for h in range(1, 4):
                merged_heads = jnp.where(lane_head == h, parts[h], merged_heads)
            picked.append(merged_heads)
        attended[i * 128 : (i + 1) * 128, :] = jnp.concatenate(picked, axis=0).astype(BF)

    def end_rows(rows_here):
        kv = project(xpad[rows_here].reshape(3 * FC, FD), FD)
        keys[rows_here] = unit_bf(kv[:, :FD]).reshape(3, FC, FD)
        vals[rows_here] = kv[:, FD:].reshape(3, FC, FD)

    hidden = w_ffn.shape[0]
    take = lax.broadcasted_iota(jnp.int32, (128, 128), 0)
    come = lax.broadcasted_iota(jnp.int32, (128, 128), 1)
    wanted = (take >> 6) * 64 + (take & 31) * 2 + ((take >> 5) & 1)
    permute = jnp.where(come == wanted, 1.0, 0.0).astype(BF)
    gain_f = gain_ffn[...]

    def feed(i):
        tokens = slice(i * 256, (i + 1) * 256)
        here = xpad[3 + 4 * i : 7 + 4 * i].reshape(256, FD).astype(F32)
        stream = here + dot(attended[tokens, :], w_proj[...])
        normed = rms(stream, gain_f)
        for c in range(0, hidden, 256):
            value = dot(normed, w_in[:, c : c + 256])
            gate = dot(normed, w_in[:, hidden + c : hidden + c + 256])
            gated = (value * jax.nn.gelu(gate)).astype(BF)
            stream = stream + dot(gated, w_ffn[c : c + 256, :])
        fine = stream.astype(BF)
        fine_out[tokens, :] = fine
        for j in range(2):
            part = dot(permute, fine[j * 128 : (j + 1) * 128]).astype(BF)
            start = (i * 2 + j) * 32
            merged[start : start + 32, :] = jnp.concatenate(
                [part[n * 32 : (n + 1) * 32] for n in range(4)], axis=1
            )

    low_half = lax.broadcasted_iota(jnp.int32, (HT, 128), 1) < HEAD
    copies = {}

    def exchange(t):
        tokens = slice(t * HT, (t + 1) * HT)
        coarse = dot(merged[tokens, :], w_merge[...]).astype(BF)
        coarse_in[tokens, :] = coarse
        normed = rms(coarse.astype(F32), gain_coarse[...])

        def heads(which):
            cols = slice(which * CD, (which + 1) * CD)
            return dot(normed, w_coarse[:, cols]).astype(BF).astype(F32)

        def unit_groups(values):
            return [unit(values[:, c : c + 256], blocks) for c in range(0, CD, 256)]

        def query_part():
            query = unit_groups(heads(0))
            for p in range(8):
                pair = query[p // 2][:, (p % 2) * 128 : (p % 2 + 1) * 128]
                turned = jnp.concatenate([pair, pair], axis=0).T
                for e in range(2):
                    first, second = turned[e * 64 : e * 64 + 32], turned[e * 64 + 32 : e * 64 + 64]
                    part = jnp.where(low_half[:32], first, second).astype(BF)
                    messages[t, 2 * p + e, HT:] = part

        def key_part():
            key = unit_groups(heads(1))
            value = heads(2)
            for p in range(8):
                k2 = key[p // 2][:, (p % 2) * 128 : (p % 2 + 1) * 128]
                v2 = value[:, p * 128 : (p + 1) * 128]
                even = jnp.where(low_half, k2, pltpu.roll(v2, HEAD, 1))
                odd = jnp.where(low_half, pltpu.roll(k2, HEAD, 1), v2)
                messages[t, 2 * p, :HT] = even.astype(BF)
                messages[t, 2 * p + 1, :HT] = odd.astype(BF)

        def send(name, rows_here, target):
            for k, (dy, dz) in enumerate(partners):
                if k != own:
                    their_head = lax.rem(y + dy, 4) * 4 + lax.rem(z + dz, 4)
                    copies[name, k] = remote(
                        messages.at[t, their_head, rows_here],
                        target(k),
                        x_send.at[name, k],
                        x_recv.at[name, k],
                        at(dy, dz),
                    )
                    copies[name, k].start()

        if t == 0:
            query_part()
            key_part()
            send(0, pl.ds(0, 96), lambda k: landed.at[k])
        else:
            query_part()
            send(1, pl.ds(HT, 32), lambda k: q_buf.at[k])
            key_part()
            send(2, pl.ds(0, HT), lambda k: kv_buf.at[2, pl.ds(k * HT, HT)])
            kv_buf[2, own * HT : (own + 1) * HT, :] = messages[1, head, :HT]

    for place in halo:
        if place != (1, 0) and place != (-1, 0):
            halo[place].wait()
    side_kv = project(side[...].reshape(SIDE, FD), FD)
    side_keys[...] = unit_bf(side_kv[:, :FD])
    side_vals[...] = side_kv[:, FD:]
    halo[1, 0].wait()
    end_rows(slice(0, 3))
    attend(0)
    attend(1)
    w_proj_load.wait()
    w_in_load.wait()
    w_ffn_load.wait()
    feed(0)
    w_merge_load.wait()
    w_coarse_load.wait()
    exchange(0)
    halo[-1, 0].wait()
    end_rows(slice(FR + 3, FR + 6))
    attend(2)
    attend(3)
    feed(1)
    exchange(1)

    q_full[HEAD:, :] = jnp.zeros((HEAD, QUERIES), BF)
    acc[...] = jnp.zeros_like(acc)
    def gather(source, target, there):
        return remote(
            kv_buf.at[source], kv_buf.at[target], g_send.at[target], g_recv.at[target], there
        )

    gathers = {
        1: gather(0, 1, sibling),
        3: gather(2, 3, sibling),
        4: gather(0, 4, up),
        5: gather(0, 5, down),
        6: gather(4, 6, sibling),
        7: gather(5, 7, sibling),
        8: gather(2, 8, up),
        9: gather(2, 9, down),
        10: gather(8, 10, sibling),
        11: gather(9, 11, sibling),
        12: gather(4, 12, up),
        13: gather(9, 13, down),
        14: gather(12, 14, sibling),
        15: gather(13, 15, sibling),
    }
    arrive = {b: ("gather", (b,)) for b in gathers}
    arrive[0] = ("plane", [(0, k) for k in range(16)])
    arrive[2] = ("plane", [(2, k) for k in range(16)])
    arrive[8] = ("gather", (8, 9))
    arrive[12] = ("gather", (12, 13))
    del arrive[9], arrive[13]
    start_after = {0: (4, 5, 1), 2: (8, 9, 3), 4: (12, 6), 5: (7,), 8: (13, 10, 11), 12: (14, 15)}

    def arrivals(b):
        kind, which = arrive[b]
        for k in which:
            if kind == "gather":
                gathers[k].wait_recv()
            elif k[1] != own:
                copies[k].wait()
        if b == 0:
            for k in range(16):
                part = messages[0, head, :HT] if k == own else landed[k, :HT]
                kv_buf[0, k * HT : (k + 1) * HT, :] = part
        for target in start_after.get(b, ()):
            gathers[target].start()

    def assemble(t):
        for k in range(0, 16, 2):
            parts = []
            for j in (k, k + 1):
                if j == own:
                    part = messages[t, head, HT:]
                elif t == 0:
                    part = landed[j, HT:]
                else:
                    copies[1, j].wait()
                    part = q_buf[j]
                parts.append(part.astype(F32))
            top = jnp.where(low_half[:32], parts[0], pltpu.roll(parts[1], HEAD, 1))
            end = jnp.where(low_half[:32], pltpu.roll(parts[0], HEAD, 1), parts[1])
            cols = slice(t * half + k * HT, t * half + (k + 2) * HT)
            q_full[0:HEAD, cols] = jnp.concatenate([top, end], axis=0).astype(BF)

    o_copies = {}
    half, quarter = QUERIES // 2, QUERIES // 4
    head_factor = scale_coarse[0, head] * (LOG2E / HEAD)
    ones = jnp.ones((8, BLOCK), BF)

    def process(b, parts):
        kv = kv_buf[b]
        lhs = jnp.concatenate([kv.T[HEAD:], ones], axis=0)
        for cols in parts:
            weights = jnp.exp2(dot(kv, q_full[:, cols]) * head_factor).astype(BF)
            acc[:, cols] += dot(lhs, weights)

    all_parts = [slice(i * quarter, (i + 1) * quarter) for i in range(4)]

    arrivals(0)
    assemble(0)
    process(0, all_parts[:2])
    arrivals(1)
    process(1, all_parts[:2])
    assemble(1)

    def step(i, carry):
        @pl.when(i < 2)
        def _():
            process(i, all_parts[2:])

        @pl.when(i >= 2)
        def _():
            for block in sorted(arrive):
                if 1 < block < 12:
                    pl.when(i == block)(lambda block=block: arrivals(block))
            process(i, [slice(0, half), slice(half, QUERIES)])

        return carry

    lax.fori_loop(0, 12, step, 0)

    low_rows = lax.broadcasted_iota(jnp.int32, (HEAD, 128), 1) < HEAD
    for first in (0, 1):
        parts = [all_parts[first], all_parts[first + 2]]

        def last(i, carry):
            if first == 0:
                pl.when(i == 0)(lambda: arrivals(12))

                @pl.when(i == 2)
                def _():
                    arrivals(14)
                    arrivals(15)

            process(12 + i, parts)
            return carry

        lax.fori_loop(0, 4, last, 0)
        done = [acc[0:HEAD, cols] * (1.0 / acc[HEAD : HEAD + 1, cols]) for cols in parts]
        for k in range(first * 8, first * 8 + 8, 2):
            start = (k - first * 8) * HT
            early, late = (half_done[:, start : start + 128] for half_done in done)
            both = (
                jnp.where(low_rows, early, pltpu.roll(late, HEAD, 1)).astype(BF),
                jnp.where(low_rows, pltpu.roll(early, HEAD, 1), late).astype(BF),
            )
            for j in (k, k + 1):
                if j == own:
                    back[head] = both[j - k]
                    continue
                dy, dz = partners[j]
                o_buf[j] = both[j - k]
                o_copies[j] = remote(
                    o_buf.at[j], back.at[head], o_send.at[j], o_recv.at[j], at(-dy, -dz)
                )
                o_copies[j].start()

    for copy in gathers.values():
        copy.wait_send()
    w_out_load.wait()
    total = coarse_in[...].astype(F32)
    for n, dy in enumerate(ORDER):
        for dz in range(4):
            if n * 4 + dz != own:
                o_copies[n * 4 + dz].wait()
        from_y = lax.rem(y + dy, 4)
        features = back[pl.ds(from_y * 4, 4)].reshape(256, CT)
        rows_here = pl.ds(pl.multiple_of(from_y * 256, 256), 256)
        total = total + lax.dot_general(
            features, w_out[rows_here, :], (((0,), (0,)), ((), ())), preferred_element_type=F32
        )
    out[...] = total.astype(BF)


def body(
    image,
    gain_attn,
    w_qkv_fine,
    scale_fine,
    w_out_fine,
    gain_ffn,
    w_ffn_in,
    w_ffn_out,
    w_merge,
    gain_coarse,
    w_qkv_coarse,
    scale_coarse,
    w_out_coarse,
):
    vmem = pl.BlockSpec(memory_space=pltpu.VMEM)
    smem = pl.BlockSpec(memory_space=pltpu.SMEM)
    hbm = pl.BlockSpec(memory_space=pl.ANY)
    dma = pltpu.SemaphoreType.DMA
    weights = (w_qkv_fine, w_out_fine, w_ffn_in, w_ffn_out, w_merge, w_qkv_coarse, w_out_coarse)
    fine_out, coarse_out = pl.pallas_call(
        kernel,
        out_shape=(pltpu.VMEM((FR * FC, FD), BF), pltpu.VMEM((CT, CD), BF)),
        in_specs=[hbm, vmem, hbm, smem, hbm, vmem, hbm, hbm, hbm, vmem, hbm, smem, hbm],
        out_specs=(vmem, vmem),
        scratch_shapes=[
            pltpu.VMEM((PR, FC, FD), BF),
            pltpu.VMEM((64, FD), BF),
            pltpu.VMEM((2, 64, FD), BF),
            pltpu.VMEM((FR * FC, FD), BF),
            pltpu.VMEM((PR, FC, FD), BF),
            pltpu.VMEM((PR, FC, FD), BF),
            pltpu.VMEM((SIDE, FD), BF),
            pltpu.VMEM((SIDE, FD), BF),
            pltpu.VMEM((8 * FC, WINDOW), F32),
            pltpu.VMEM((8 * FC, SIDE), jnp.int32),
            pltpu.VMEM((FR * FC, FD), BF),
            pltpu.VMEM((CT, CD), BF),
            pltpu.VMEM((CT, CD), BF),
            pltpu.VMEM((2, NHEAD, HT + HEAD // 2, 128), BF),
            pltpu.VMEM((NHEAD, HT + HEAD // 2, 128), BF),
            pltpu.VMEM((NBLOCK, BLOCK, 128), BF),
            pltpu.VMEM((NHEAD, HEAD // 2, 128), BF),
            pltpu.VMEM((128, QUERIES), BF),
            pltpu.VMEM((HEAD + 8, QUERIES), F32),
            pltpu.VMEM((NHEAD, HEAD, CT), BF),
            pltpu.VMEM((NHEAD, HEAD, CT), BF),
        ]
        + [pltpu.VMEM(w.shape, BF) for w in weights]
        + [dma((8,)), dma((8,)), dma((8,))]
        + [dma((3, 16))] * 2
        + [dma((16,))] * 4,
        compiler_params=pltpu.CompilerParams(
            collective_id=0, has_side_effects=True, vmem_limit_bytes=VMEM_LIMIT
        ),
        name="window",
    )(
        image,
        gain_attn.reshape(1, -1),
        w_qkv_fine,
        scale_fine.reshape(1, -1),
        w_out_fine,
        gain_ffn.reshape(1, -1),
        w_ffn_in,
        w_ffn_out,
        w_merge,
        gain_coarse.reshape(1, -1),
        w_qkv_coarse,
        scale_coarse.reshape(1, -1),
        w_out_coarse,
    )
    return fine_out.reshape(image.shape), coarse_out.reshape(FR // 2, FC // 2, CD)


def solution(mesh):
    placed = (P("rows", "seq", None),) + (P(),) * 12
    return jax.shard_map(
        body,
        mesh=mesh,
        in_specs=placed,
        out_specs=(P("rows", "seq", None), P("rows", "seq", None)),
        check_vma=False,
    )
```

```python
import math

import jax
import jax.numpy as jnp
from jax import lax
from jax.experimental import pallas as pl
from jax.experimental.pallas import tpu as pltpu
from jax.sharding import PartitionSpec as P

HEAD = 64
MESH = pl.DeviceIdType.MESH
BF = jnp.bfloat16
F32 = jnp.float32
LOG2E = math.log2(math.e)

FR, FC, FD = 8, 64, 256
PR = FR + 6
OWN = FR * FC
SIDE = 128
HALO = SIDE + 3 * FC
CT, CD = 128, 1024
NHEAD = 16
HT = CT // 2
QUERIES = NHEAD * CT
BLOCK = 1024
NBLOCK = 16
ORDER = (1, 2, 3, 0)
VMEM_LIMIT = 56 * 2**20


def rms(values, gain):
    mean_square = jnp.mean(values * values, axis=-1, keepdims=True)
    return (values * lax.rsqrt(mean_square + 1e-06) * gain).astype(BF)


def dot(a, b):
    return jnp.dot(a, b, preferred_element_type=F32)


def unit(values, blocks):
    square = values * values
    high = square.astype(BF)
    low = (square - high.astype(F32)).astype(BF)
    return values * lax.rsqrt(dot(high, blocks) + dot(low, blocks) + 1e-06)


def kernel(
    image,
    gain_attn_hbm,
    w_qkv_hbm,
    scale_fine_hbm,
    w_proj_hbm,
    gain_ffn_hbm,
    w_in_hbm,
    w_ffn_hbm,
    w_merge_hbm,
    gain_coarse_hbm,
    w_coarse_hbm,
    scale_coarse_hbm,
    w_out_hbm,
    fine_out,
    out,
    xpad,
    packed,
    side,
    keys,
    vals,
    halo_keys,
    halo_vals,
    bias,
    halo_gap,
    stacked,
    own_total,
    own_sum,
    attended,
    merged,
    coarse_in,
    messages,
    landed,
    kv_buf,
    q_buf,
    q_full,
    acc,
    o_buf,
    back,
    w_qkv,
    w_proj,
    w_in,
    w_ffn,
    w_merge,
    w_coarse,
    w_out,
    gain_attn,
    gain_ffn,
    gain_coarse,
    scale_fine,
    scale_coarse,
    load_sem,
    halo_send,
    halo_recv,
    x_send,
    x_recv,
    g_send,
    g_recv,
    o_send,
    o_recv,
):
    row, seq = lax.axis_index("rows"), lax.axis_index("seq")
    n_rows, n_seq = lax.axis_size("rows"), lax.axis_size("seq")
    x, y, z_lo = row // 8, lax.rem(row // 2, 4), lax.rem(row, 2)
    z_hi, core = seq // 2, lax.rem(seq, 2)
    z = z_hi * 2 + z_lo
    head = y * 4 + z

    def at(dy, dz):
        py, pz = lax.rem(y + dy + 4, 4), lax.rem(z + dz + 4, 4)
        return (x * 8 + py * 2 + lax.rem(pz, 2), (pz // 2) * 2 + core)

    def beside(dr, ds):
        return (lax.rem(row + dr + n_rows, n_rows), lax.rem(seq + ds + n_seq, n_seq))

    sibling = (row, seq + 1 - 2 * core)
    up = (lax.rem(row + 8, 32), seq)
    down = (lax.rem(row + 24, 32), seq)
    around = [(dr, ds) for dr in (0, -1, 1) for ds in (0, -1, 1) if (dr, ds) != (0, 0)]
    partners = [(dy, dz) for dy in ORDER for dz in range(4)]
    own = partners.index((0, 0))

    def load(source, target, i):
        copy = pltpu.make_async_copy(source, target, load_sem.at[i])
        copy.start()
        return copy

    image_load = load(image, xpad.at[pl.ds(3, FR)], 0)
    barrier = pltpu.get_barrier_semaphore()
    everyone = [beside(dr, ds) for dr, ds in around]
    everyone += [at(dy, dz) for k, (dy, dz) in enumerate(partners) if k != own]
    everyone += [sibling, up, down]
    for there in everyone:
        pl.semaphore_signal(barrier, inc=1, device_id=there, device_id_type=MESH)

    w_qkv_load = load(w_qkv_hbm, w_qkv, 1)
    small_loads = [
        load(gain_attn_hbm, gain_attn, 8),
        load(gain_ffn_hbm, gain_ffn, 9),
        load(gain_coarse_hbm, gain_coarse, 10),
        load(scale_fine_hbm, scale_fine, 11),
        load(scale_coarse_hbm, scale_coarse, 12),
    ]
    w_proj_load = load(w_proj_hbm, w_proj, 2)
    w_in_load = load(w_in_hbm, w_in, 3)
    w_ffn_load = load(w_ffn_hbm, w_ffn, 4)
    w_merge_load = load(w_merge_hbm, w_merge, 5)
    w_coarse_load = load(w_coarse_hbm, w_coarse, 6)
    w_out_load = load(w_out_hbm, w_out, 7)

    def remote(src, dst, send, recv, there):
        return pltpu.make_async_remote_copy(
            src_ref=src,
            dst_ref=dst,
            send_sem=send,
            recv_sem=recv,
            device_id=there,
            device_id_type=MESH,
        )

    image_load.wait()
    pl.semaphore_wait(barrier, len(everyone))

    halo = {}

    def send_halo(place, source, target):
        i = len(halo)
        halo[place] = remote(source, target, halo_send.at[i], halo_recv.at[i], beside(*place))
        halo[place].start()

    send_halo((1, 0), xpad.at[pl.ds(FR, 3)], xpad.at[pl.ds(0, 3)])
    take = lax.broadcasted_iota(jnp.int32, (64, FR * FC), 0)
    come = lax.broadcasted_iota(jnp.int32, (64, FR * FC), 1)
    wanted = ((take & 31) >> 2) * FC + (take & 3) + (take >> 5) * (FC - 4)
    pick = jnp.where(come == wanted, 1.0, 0.0).astype(BF)
    packed[...] = dot(pick, xpad[3 : 3 + FR].reshape(FR * FC, FD)).astype(BF)
    for ds, start in ((-1, 0), (1, 32)):
        there = 1 if ds == -1 else 0
        send_halo((0, ds), packed.at[pl.ds(start, 32)], side.at[there, pl.ds(16, 32)])
        send_halo((-1, ds), packed.at[pl.ds(start, 16)], side.at[there, pl.ds(48, 16)])
        send_halo((1, ds), packed.at[pl.ds(start + 16, 16)], side.at[there, pl.ds(0, 16)])
    send_halo((-1, 0), xpad.at[pl.ds(3, 3)], xpad.at[pl.ds(FR + 3, 3)])

    group = (lax.broadcasted_iota(jnp.int32, (FD, FD), 0) >> 6) == (
        lax.broadcasted_iota(jnp.int32, (FD, FD), 1) >> 6
    )
    blocks = jnp.where(group, 1.0 / HEAD, 0.0).astype(BF)
    w_qkv_load.wait()
    for copy in small_loads:
        copy.wait()
    gain = gain_attn[...]

    def project(tokens, first):
        normed = rms(tokens.astype(F32), gain)
        return dot(normed, w_qkv[:, first:]).astype(BF)

    def unit_bf(values):
        return unit(values.astype(F32), blocks).astype(BF)

    lane_head = lax.broadcasted_iota(jnp.int32, (FC, FD), 1) >> 6
    for i in range(2):
        tokens = slice(i * 256, (i + 1) * 256)
        triple = project(xpad[3 + 4 * i : 7 + 4 * i].reshape(256, FD), 0)
        query = unit(triple[:, :FD].astype(F32), blocks)
        for r in range(4):
            for h in range(4):
                one = jnp.where(lane_head == h, query[r * FC : (r + 1) * FC], 0.0)
                start = ((r % 2) * 4 + h) * FC
                stacked[i * 2 + r // 2, start : start + FC, :] = one.astype(BF)
        keys[tokens, :] = unit_bf(triple[:, FD : 2 * FD])
        vals[tokens, :] = triple[:, 2 * FD :]

    query_col = lax.broadcasted_iota(jnp.int32, (FC, OWN), 0)
    gap = (lax.broadcasted_iota(jnp.int32, (FC, OWN), 1) & 63) - query_col
    near = jnp.where((gap >= -3) & (gap <= 3), 0.0, -1e30).astype(F32)
    bias[...] = jnp.concatenate([near] * 4, axis=0)
    own_row = lax.broadcasted_iota(jnp.int32, (1, OWN), 1) >> 6
    factor = jnp.concatenate(
        [
            jnp.broadcast_to(scale_fine[0:1, h : h + 1] * (LOG2E / HEAD), (FC, 1))
            for h in range(4)
        ],
        axis=0,
    )
    factors = jnp.concatenate([factor, factor], axis=0)
    last_dims = (((1,), (1,)), ((), ()))

    def attend_own(i):
        scores = lax.dot_general(
            stacked[i], keys[...], last_dims, preferred_element_type=F32
        )
        weights = []
        for r in range(2):
            off = own_row + 3 - r - 2 * i
            row_bias = jnp.where((off >= 0) & (off <= 6), 0.0, -1e30).astype(F32)
            part = scores[r * 256 : (r + 1) * 256] * factor + (bias[...] + row_bias)
            weights.append(jnp.exp2(part))
        weights = jnp.concatenate(weights, axis=0)
        own_total[i] = dot(weights.astype(BF), vals[...])
        weight_sum = weights[:, :128]
        for j in range(128, OWN, 128):
            weight_sum = weight_sum + weights[:, j : j + 128]
        own_sum[i] = weight_sum

    query_col = lax.broadcasted_iota(jnp.int32, (FC, HALO), 0)
    slot = lax.broadcasted_iota(jnp.int32, (FC, HALO), 1)
    beyond = slot - SIDE
    right = slot >> 6
    for t in range(2):
        key_row = jnp.where(slot < SIDE, ((slot & 63) >> 2) - 1, (beyond >> 6) + t * (FR + 3))
        key_col = jnp.where(slot < SIDE, (slot & 3) - 4 + right * (FC + 4), beyond & 63)
        global_row = row * FR + key_row - 3
        global_col = seq * FC + key_col
        inside = (global_row >= 0) & (global_row < n_rows * FR)
        inside = inside & (global_col >= 0) & (global_col < n_seq * FC)
        inside = inside & (key_col - query_col >= -3) & (key_col - query_col <= 3)
        gap = jnp.where(inside, key_row, 1000)
        for r in range(2):
            for h in range(4):
                start = (r * 4 + h) * FC
                halo_gap[t, start : start + FC, :] = gap - r

    for i in range(4):
        attend_own(i)

    def attend(i):
        t = i // 2
        scores = lax.dot_general(
            stacked[i], halo_keys[t], last_dims, preferred_element_type=F32
        )
        off = halo_gap[t] - i * 2
        weights = jnp.where((off >= 0) & (off <= 6), jnp.exp2(scores * factors), 0.0)
        total = own_total[i] + dot(weights.astype(BF), halo_vals[t])
        weight_sum = jnp.sum(own_sum[i], axis=-1, keepdims=True) + jnp.sum(
            weights, axis=-1, keepdims=True
        )
        scaled = total * (1.0 / weight_sum)
        picked = []
        for r in range(2):
            parts = [scaled[(r * 4 + h) * FC : (r * 4 + h + 1) * FC] for h in range(4)]
            merged_heads = parts[0]
            for h in range(1, 4):
                merged_heads = jnp.where(lane_head == h, parts[h], merged_heads)
            picked.append(merged_heads)
        attended[i * 128 : (i + 1) * 128, :] = jnp.concatenate(picked, axis=0).astype(BF)

    def end_rows(t, rows_here):
        kv = project(xpad[rows_here].reshape(3 * FC, FD), FD)
        halo_keys[t, SIDE:, :] = unit_bf(kv[:, :FD])
        halo_vals[t, SIDE:, :] = kv[:, FD:]

    hidden = w_ffn.shape[0]
    take = lax.broadcasted_iota(jnp.int32, (128, 128), 0)
    come = lax.broadcasted_iota(jnp.int32, (128, 128), 1)
    wanted = (take >> 6) * 64 + (take & 31) * 2 + ((take >> 5) & 1)
    permute = jnp.where(come == wanted, 1.0, 0.0).astype(BF)
    gain_f = gain_ffn[...]

    def feed(i):
        tokens = slice(i * 256, (i + 1) * 256)
        here = xpad[3 + 4 * i : 7 + 4 * i].reshape(256, FD).astype(F32)
        stream = here + dot(attended[tokens, :], w_proj[...])
        normed = rms(stream, gain_f)
        for c in range(0, hidden, 256):
            value = dot(normed, w_in[:, c : c + 256])
            gate = dot(normed, w_in[:, hidden + c : hidden + c + 256])
            gated = (value * jax.nn.gelu(gate)).astype(BF)
            stream = stream + dot(gated, w_ffn[c : c + 256, :])
        fine = stream.astype(BF)
        fine_out[tokens, :] = fine
        for j in range(2):
            part = dot(permute, fine[j * 128 : (j + 1) * 128]).astype(BF)
            start = (i * 2 + j) * 32
            merged[start : start + 32, :] = jnp.concatenate(
                [part[n * 32 : (n + 1) * 32] for n in range(4)], axis=1
            )

    low_half = lax.broadcasted_iota(jnp.int32, (HT, 128), 1) < HEAD
    copies = {}

    def exchange(t):
        tokens = slice(t * HT, (t + 1) * HT)
        coarse = dot(merged[tokens, :], w_merge[...]).astype(BF)
        coarse_in[tokens, :] = coarse
        normed = rms(coarse.astype(F32), gain_coarse[...])

        def heads(which):
            cols = slice(which * CD, (which + 1) * CD)
            return dot(normed, w_coarse[:, cols]).astype(BF).astype(F32)

        def unit_groups(values):
            return [unit(values[:, c : c + 256], blocks) for c in range(0, CD, 256)]

        def query_part():
            query = unit_groups(heads(0))
            for p in range(8):
                pair = query[p // 2][:, (p % 2) * 128 : (p % 2 + 1) * 128]
                turned = jnp.concatenate([pair, pair], axis=0).T
                for e in range(2):
                    first, second = turned[e * 64 : e * 64 + 32], turned[e * 64 + 32 : e * 64 + 64]
                    part = jnp.where(low_half[:32], first, second).astype(BF)
                    messages[t, 2 * p + e, HT:] = part

        def key_part():
            key = unit_groups(heads(1))
            value = heads(2)
            for p in range(8):
                k2 = key[p // 2][:, (p % 2) * 128 : (p % 2 + 1) * 128]
                v2 = value[:, p * 128 : (p + 1) * 128]
                even = jnp.where(low_half, k2, pltpu.roll(v2, HEAD, 1))
                odd = jnp.where(low_half, pltpu.roll(k2, HEAD, 1), v2)
                messages[t, 2 * p, :HT] = even.astype(BF)
                messages[t, 2 * p + 1, :HT] = odd.astype(BF)

        def send(name, rows_here, target):
            for k, (dy, dz) in enumerate(partners):
                if k != own:
                    their_head = lax.rem(y + dy, 4) * 4 + lax.rem(z + dz, 4)
                    copies[name, k] = remote(
                        messages.at[t, their_head, rows_here],
                        target(k),
                        x_send.at[name, k],
                        x_recv.at[name, k],
                        at(dy, dz),
                    )
                    copies[name, k].start()

        if t == 0:
            query_part()
            key_part()
            send(0, pl.ds(0, 96), lambda k: landed.at[k])
        else:
            query_part()
            send(1, pl.ds(HT, 32), lambda k: q_buf.at[k])
            key_part()
            send(2, pl.ds(0, HT), lambda k: kv_buf.at[2, pl.ds(k * HT, HT)])
            kv_buf[2, own * HT : (own + 1) * HT, :] = messages[1, head, :HT]

    for place in halo:
        if place != (1, 0) and place != (-1, 0):
            halo[place].wait()
    side_kv = project(side[...].reshape(SIDE, FD), FD)
    side_keys = unit_bf(side_kv[:, :FD])
    for t in range(2):
        halo_keys[t, :SIDE, :] = side_keys
        halo_vals[t, :SIDE, :] = side_kv[:, FD:]
    halo[1, 0].wait()
    end_rows(0, slice(0, 3))
    attend(0)
    attend(1)
    w_proj_load.wait()
    w_in_load.wait()
    w_ffn_load.wait()
    feed(0)
    w_merge_load.wait()
    w_coarse_load.wait()
    exchange(0)
    halo[-1, 0].wait()
    end_rows(1, slice(FR + 3, FR + 6))
    attend(2)
    attend(3)
    feed(1)
    exchange(1)

    q_full[HEAD:, :] = jnp.zeros((HEAD, QUERIES), BF)
    acc[...] = jnp.zeros_like(acc)
    def gather(source, target, there):
        return remote(
            kv_buf.at[source], kv_buf.at[target], g_send.at[target], g_recv.at[target], there
        )

    gathers = {
        1: gather(0, 1, sibling),
        3: gather(2, 3, sibling),
        4: gather(0, 4, up),
        5: gather(0, 5, down),
        6: gather(4, 6, sibling),
        7: gather(5, 7, sibling),
        8: gather(2, 8, up),
        9: gather(2, 9, down),
        10: gather(8, 10, sibling),
        11: gather(9, 11, sibling),
        12: gather(4, 12, up),
        13: gather(9, 13, down),
        14: gather(12, 14, sibling),
        15: gather(13, 15, sibling),
    }
    arrive = {b: ("gather", (b,)) for b in gathers}
    arrive[0] = ("plane", [(0, k) for k in range(16)])
    arrive[2] = ("plane", [(2, k) for k in range(16)])
    arrive[8] = ("gather", (8, 9))
    arrive[12] = ("gather", (12, 13))
    del arrive[9], arrive[13]
    start_after = {0: (4, 5, 1), 2: (8, 9, 3), 4: (12, 6), 5: (7,), 8: (13, 10, 11), 12: (14, 15)}

    def arrivals(b):
        kind, which = arrive[b]
        for k in which:
            if kind == "gather":
                gathers[k].wait_recv()
            elif k[1] != own:
                copies[k].wait()
        if b == 0:
            for k in range(16):
                part = messages[0, head, :HT] if k == own else landed[k, :HT]
                kv_buf[0, k * HT : (k + 1) * HT, :] = part
        for target in start_after.get(b, ()):
            gathers[target].start()

    def assemble(t):
        for k in range(0, 16, 2):
            parts = []
            for j in (k, k + 1):
                if j == own:
                    part = messages[t, head, HT:]
                elif t == 0:
                    part = landed[j, HT:]
                else:
                    copies[1, j].wait()
                    part = q_buf[j]
                parts.append(part.astype(F32))
            top = jnp.where(low_half[:32], parts[0], pltpu.roll(parts[1], HEAD, 1))
            end = jnp.where(low_half[:32], pltpu.roll(parts[0], HEAD, 1), parts[1])
            cols = slice(t * half + k * HT, t * half + (k + 2) * HT)
            q_full[0:HEAD, cols] = jnp.concatenate([top, end], axis=0).astype(BF)

    o_copies = {}
    half, quarter = QUERIES // 2, QUERIES // 4
    of_head = lax.broadcasted_iota(jnp.int32, (1, NHEAD), 1) == head
    head_scale = jnp.sum(jnp.where(of_head, scale_coarse[...], 0.0), axis=1, keepdims=True)
    head_factor = head_scale * (LOG2E / HEAD)
    ones = jnp.ones((8, BLOCK), BF)

    def process(b, parts):
        kv = kv_buf[b]
        lhs = jnp.concatenate([kv.T[HEAD:], ones], axis=0)
        for cols in parts:
            weights = jnp.exp2(dot(kv, q_full[:, cols]) * head_factor).astype(BF)
            acc[:, cols] += dot(lhs, weights)

    all_parts = [slice(i * quarter, (i + 1) * quarter) for i in range(4)]

    arrivals(0)
    assemble(0)
    process(0, all_parts[:2])
    arrivals(1)
    process(1, all_parts[:2])
    assemble(1)

    def step(i, carry):
        @pl.when(i < 2)
        def _():
            process(i, all_parts[2:])

        @pl.when(i >= 2)
        def _():
            for block in sorted(arrive):
                if 1 < block < 12:
                    pl.when(i == block)(lambda block=block: arrivals(block))
            process(i, [slice(0, half), slice(half, QUERIES)])

        return carry

    lax.fori_loop(0, 12, step, 0)

    low_rows = lax.broadcasted_iota(jnp.int32, (HEAD, 128), 1) < HEAD
    for first in (0, 1):
        parts = [all_parts[first], all_parts[first + 2]]

        def last(i, carry):
            if first == 0:
                pl.when(i == 0)(lambda: arrivals(12))

                @pl.when(i == 2)
                def _():
                    arrivals(14)
                    arrivals(15)

            process(12 + i, parts)
            return carry

        lax.fori_loop(0, 4, last, 0)
        done = [acc[0:HEAD, cols] * (1.0 / acc[HEAD : HEAD + 1, cols]) for cols in parts]
        for k in range(first * 8, first * 8 + 8, 2):
            start = (k - first * 8) * HT
            early, late = (half_done[:, start : start + 128] for half_done in done)
            both = (
                jnp.where(low_rows, early, pltpu.roll(late, HEAD, 1)).astype(BF),
                jnp.where(low_rows, pltpu.roll(early, HEAD, 1), late).astype(BF),
            )
            for j in (k, k + 1):
                if j == own:
                    back[head] = both[j - k]
                    continue
                dy, dz = partners[j]
                o_buf[j] = both[j - k]
                o_copies[j] = remote(
                    o_buf.at[j], back.at[head], o_send.at[j], o_recv.at[j], at(-dy, -dz)
                )
                o_copies[j].start()

    for copy in gathers.values():
        copy.wait_send()
    w_out_load.wait()
    total = coarse_in[...].astype(F32)
    for n, dy in enumerate(ORDER):
        for dz in range(4):
            if n * 4 + dz != own:
                o_copies[n * 4 + dz].wait()
        from_y = lax.rem(y + dy, 4)
        features = back[pl.ds(from_y * 4, 4)].reshape(256, CT)
        rows_here = pl.ds(pl.multiple_of(from_y * 256, 256), 256)
        total = total + lax.dot_general(
            features, w_out[rows_here, :], (((0,), (0,)), ((), ())), preferred_element_type=F32
        )
    out[...] = total.astype(BF)


def body(
    image,
    gain_attn,
    w_qkv_fine,
    scale_fine,
    w_out_fine,
    gain_ffn,
    w_ffn_in,
    w_ffn_out,
    w_merge,
    gain_coarse,
    w_qkv_coarse,
    scale_coarse,
    w_out_coarse,
):
    vmem = pl.BlockSpec(memory_space=pltpu.VMEM)
    hbm = pl.BlockSpec(memory_space=pl.ANY)
    dma = pltpu.SemaphoreType.DMA
    weights = (w_qkv_fine, w_out_fine, w_ffn_in, w_ffn_out, w_merge, w_qkv_coarse, w_out_coarse)
    fine_out, coarse_out = pl.pallas_call(
        kernel,
        out_shape=(pltpu.VMEM((FR * FC, FD), BF), pltpu.VMEM((CT, CD), BF)),
        in_specs=[hbm] * 13,
        out_specs=(vmem, vmem),
        scratch_shapes=[
            pltpu.VMEM((PR, FC, FD), BF),
            pltpu.VMEM((64, FD), BF),
            pltpu.VMEM((2, 64, FD), BF),
            pltpu.VMEM((OWN, FD), BF),
            pltpu.VMEM((OWN, FD), BF),
            pltpu.VMEM((2, HALO, FD), BF),
            pltpu.VMEM((2, HALO, FD), BF),
            pltpu.VMEM((4 * FC, OWN), F32),
            pltpu.VMEM((2, 8 * FC, HALO), jnp.int32),
            pltpu.VMEM((4, 8 * FC, FD), BF),
            pltpu.VMEM((4, 8 * FC, FD), F32),
            pltpu.VMEM((4, 8 * FC, 128), F32),
            pltpu.VMEM((FR * FC, FD), BF),
            pltpu.VMEM((CT, CD), BF),
            pltpu.VMEM((CT, CD), BF),
            pltpu.VMEM((2, NHEAD, HT + HEAD // 2, 128), BF),
            pltpu.VMEM((NHEAD, HT + HEAD // 2, 128), BF),
            pltpu.VMEM((NBLOCK, BLOCK, 128), BF),
            pltpu.VMEM((NHEAD, HEAD // 2, 128), BF),
            pltpu.VMEM((128, QUERIES), BF),
            pltpu.VMEM((HEAD + 8, QUERIES), F32),
            pltpu.VMEM((NHEAD, HEAD, CT), BF),
            pltpu.VMEM((NHEAD, HEAD, CT), BF),
        ]
        + [pltpu.VMEM(w.shape, BF) for w in weights]
        + [pltpu.VMEM((1, n), F32) for n in (FD, FD, CD, 4, NHEAD)]
        + [dma((13,)), dma((8,)), dma((8,))]
        + [dma((3, 16))] * 2
        + [dma((16,))] * 4,
        compiler_params=pltpu.CompilerParams(
            collective_id=0, has_side_effects=True, vmem_limit_bytes=VMEM_LIMIT
        ),
        name="window",
    )(
        image,
        gain_attn.reshape(1, -1),
        w_qkv_fine,
        scale_fine.reshape(1, -1),
        w_out_fine,
        gain_ffn.reshape(1, -1),
        w_ffn_in,
        w_ffn_out,
        w_merge,
        gain_coarse.reshape(1, -1),
        w_qkv_coarse,
        scale_coarse.reshape(1, -1),
        w_out_coarse,
    )
    return fine_out.reshape(image.shape), coarse_out.reshape(FR // 2, FC // 2, CD)


def solution(mesh):
    placed = (P("rows", "seq", None),) + (P(),) * 12
    return jax.shard_map(
        body,
        mesh=mesh,
        in_specs=placed,
        out_specs=(P("rows", "seq", None), P("rows", "seq", None)),
        check_vma=False,
    )
```

```python
import math

import jax
import jax.numpy as jnp
from jax import lax
from jax.experimental import pallas as pl
from jax.experimental.pallas import tpu as pltpu
from jax.sharding import PartitionSpec as P

HEAD = 64
MESH = pl.DeviceIdType.MESH
BF = jnp.bfloat16
F32 = jnp.float32
LOG2E = math.log2(math.e)

FR, FC, FD = 8, 64, 256
PR = FR + 6
OWN = FR * FC
SIDE = 128
HALO = SIDE + 3 * FC
CT, CD = 128, 1024
NHEAD = 16
HT = CT // 2
QUERIES = NHEAD * CT
BLOCK = 1024
NBLOCK = 16
ORDER = (1, 2, 3, 0)
VMEM_LIMIT = 56 * 2**20


def rms(values, gain):
    mean_square = jnp.mean(values * values, axis=-1, keepdims=True)
    return (values * lax.rsqrt(mean_square + 1e-06) * gain).astype(BF)


def dot(a, b):
    return jnp.dot(a, b, preferred_element_type=F32)


def unit(values, blocks):
    square = values * values
    high = square.astype(BF)
    low = (square - high.astype(F32)).astype(BF)
    return values * lax.rsqrt(dot(high, blocks) + dot(low, blocks) + 1e-06)


def kernel(
    image,
    gain_attn_hbm,
    w_qkv_hbm,
    scale_fine_hbm,
    w_proj_hbm,
    gain_ffn_hbm,
    w_in_hbm,
    w_ffn_hbm,
    w_merge_hbm,
    gain_coarse_hbm,
    w_coarse_hbm,
    scale_coarse_hbm,
    w_out_hbm,
    fine_out,
    out,
    xpad,
    packed,
    side,
    keys,
    vals,
    halo_keys,
    halo_vals,
    bias,
    halo_gap,
    stacked,
    own_total,
    own_sum,
    attended,
    merged,
    coarse_in,
    messages,
    landed,
    kv_buf,
    q_buf,
    q_full,
    acc,
    o_buf,
    back,
    w_qkv,
    w_proj,
    w_in,
    w_ffn,
    w_merge,
    w_coarse,
    w_out,
    gain_attn,
    gain_ffn,
    gain_coarse,
    scale_fine,
    scale_coarse,
    load_sem,
    halo_send,
    halo_recv,
    x_send,
    x_recv,
    g_send,
    g_recv,
    o_send,
    o_recv,
):
    row, seq = lax.axis_index("rows"), lax.axis_index("seq")
    n_rows, n_seq = lax.axis_size("rows"), lax.axis_size("seq")
    x, y, z_lo = row // 8, lax.rem(row // 2, 4), lax.rem(row, 2)
    z_hi, core = seq // 2, lax.rem(seq, 2)
    z = z_hi * 2 + z_lo
    head = y * 4 + z

    def at(dy, dz):
        py, pz = lax.rem(y + dy + 4, 4), lax.rem(z + dz + 4, 4)
        return (x * 8 + py * 2 + lax.rem(pz, 2), (pz // 2) * 2 + core)

    def beside(dr, ds):
        return (lax.rem(row + dr + n_rows, n_rows), lax.rem(seq + ds + n_seq, n_seq))

    sibling = (row, seq + 1 - 2 * core)
    up = (lax.rem(row + 8, 32), seq)
    down = (lax.rem(row + 24, 32), seq)
    around = [(dr, ds) for dr in (0, -1, 1) for ds in (0, -1, 1) if (dr, ds) != (0, 0)]
    partners = [(dy, dz) for dy in ORDER for dz in range(4)]
    own = partners.index((0, 0))
    hops = (0, 1, 2, 1)
    farthest = sorted(range(16), key=lambda k: -hops[partners[k][0]] - hops[partners[k][1]])
    farthest.remove(own)

    def load(source, target, i):
        copy = pltpu.make_async_copy(source, target, load_sem.at[i])
        copy.start()
        return copy

    image_load = load(image, xpad.at[pl.ds(3, FR)], 0)
    barrier = pltpu.get_barrier_semaphore()
    everyone = [beside(dr, ds) for dr, ds in around]
    everyone += [at(dy, dz) for k, (dy, dz) in enumerate(partners) if k != own]
    everyone += [sibling, up, down]
    for there in everyone:
        pl.semaphore_signal(barrier, inc=1, device_id=there, device_id_type=MESH)

    w_qkv_load = load(w_qkv_hbm, w_qkv, 1)
    small_loads = [
        load(gain_attn_hbm, gain_attn, 8),
        load(gain_ffn_hbm, gain_ffn, 9),
        load(gain_coarse_hbm, gain_coarse, 10),
        load(scale_fine_hbm, scale_fine, 11),
        load(scale_coarse_hbm, scale_coarse, 12),
    ]
    w_proj_load = load(w_proj_hbm, w_proj, 2)
    w_in_load = load(w_in_hbm, w_in, 3)
    w_ffn_load = load(w_ffn_hbm, w_ffn, 4)
    w_merge_load = load(w_merge_hbm, w_merge, 5)
    w_coarse_load = load(w_coarse_hbm, w_coarse, 6)
    w_out_load = load(w_out_hbm, w_out, 7)

    def remote(src, dst, send, recv, there):
        return pltpu.make_async_remote_copy(
            src_ref=src,
            dst_ref=dst,
            send_sem=send,
            recv_sem=recv,
            device_id=there,
            device_id_type=MESH,
        )

    image_load.wait()
    pl.semaphore_wait(barrier, len(everyone))

    halo = {}

    def send_halo(place, source, target):
        i = len(halo)
        halo[place] = remote(source, target, halo_send.at[i], halo_recv.at[i], beside(*place))
        halo[place].start()

    send_halo((1, 0), xpad.at[pl.ds(FR, 3)], xpad.at[pl.ds(0, 3)])
    take = lax.broadcasted_iota(jnp.int32, (64, FR * FC), 0)
    come = lax.broadcasted_iota(jnp.int32, (64, FR * FC), 1)
    wanted = ((take & 31) >> 2) * FC + (take & 3) + (take >> 5) * (FC - 4)
    pick = jnp.where(come == wanted, 1.0, 0.0).astype(BF)
    packed[...] = dot(pick, xpad[3 : 3 + FR].reshape(FR * FC, FD)).astype(BF)
    for ds, start in ((-1, 0), (1, 32)):
        there = 1 if ds == -1 else 0
        send_halo((0, ds), packed.at[pl.ds(start, 32)], side.at[there, pl.ds(16, 32)])
        send_halo((-1, ds), packed.at[pl.ds(start, 16)], side.at[there, pl.ds(48, 16)])
        send_halo((1, ds), packed.at[pl.ds(start + 16, 16)], side.at[there, pl.ds(0, 16)])
    send_halo((-1, 0), xpad.at[pl.ds(3, 3)], xpad.at[pl.ds(FR + 3, 3)])

    group = (lax.broadcasted_iota(jnp.int32, (FD, FD), 0) >> 6) == (
        lax.broadcasted_iota(jnp.int32, (FD, FD), 1) >> 6
    )
    blocks = jnp.where(group, 1.0 / HEAD, 0.0).astype(BF)
    w_qkv_load.wait()
    for copy in small_loads:
        copy.wait()
    gain = gain_attn[...]

    def project(tokens, first):
        normed = rms(tokens.astype(F32), gain)
        return dot(normed, w_qkv[:, first:]).astype(BF)

    def unit_bf(values):
        return unit(values.astype(F32), blocks).astype(BF)

    lane_head = lax.broadcasted_iota(jnp.int32, (FC, FD), 1) >> 6
    for i in range(2):
        tokens = slice(i * 256, (i + 1) * 256)
        triple = project(xpad[3 + 4 * i : 7 + 4 * i].reshape(256, FD), 0)
        query = unit(triple[:, :FD].astype(F32), blocks)
        for r in range(4):
            for h in range(4):
                one = jnp.where(lane_head == h, query[r * FC : (r + 1) * FC], 0.0)
                start = ((r % 2) * 4 + h) * FC
                stacked[i * 2 + r // 2, start : start + FC, :] = one.astype(BF)
        keys[tokens, :] = unit_bf(triple[:, FD : 2 * FD])
        vals[tokens, :] = triple[:, 2 * FD :]

    query_col = lax.broadcasted_iota(jnp.int32, (FC, OWN), 0)
    gap = (lax.broadcasted_iota(jnp.int32, (FC, OWN), 1) & 63) - query_col
    near = jnp.where((gap >= -3) & (gap <= 3), 0.0, -1e30).astype(F32)
    bias[...] = jnp.concatenate([near] * 4, axis=0)
    own_row = lax.broadcasted_iota(jnp.int32, (1, OWN), 1) >> 6
    factor = jnp.concatenate(
        [
            jnp.broadcast_to(scale_fine[0:1, h : h + 1] * (LOG2E / HEAD), (FC, 1))
            for h in range(4)
        ],
        axis=0,
    )
    factors = jnp.concatenate([factor, factor], axis=0)
    last_dims = (((1,), (1,)), ((), ()))

    def attend_own(i):
        scores = lax.dot_general(
            stacked[i], keys[...], last_dims, preferred_element_type=F32
        )
        weights = []
        for r in range(2):
            off = own_row + 3 - r - 2 * i
            row_bias = jnp.where((off >= 0) & (off <= 6), 0.0, -1e30).astype(F32)
            part = scores[r * 256 : (r + 1) * 256] * factor + (bias[...] + row_bias)
            weights.append(jnp.exp2(part))
        weights = jnp.concatenate(weights, axis=0)
        own_total[i] = dot(weights.astype(BF), vals[...])
        weight_sum = weights[:, :128]
        for j in range(128, OWN, 128):
            weight_sum = weight_sum + weights[:, j : j + 128]
        own_sum[i] = weight_sum

    query_col = lax.broadcasted_iota(jnp.int32, (FC, HALO), 0)
    slot = lax.broadcasted_iota(jnp.int32, (FC, HALO), 1)
    beyond = slot - SIDE
    right = slot >> 6
    for t in range(2):
        key_row = jnp.where(slot < SIDE, ((slot & 63) >> 2) - 1, (beyond >> 6) + t * (FR + 3))
        key_col = jnp.where(slot < SIDE, (slot & 3) - 4 + right * (FC + 4), beyond & 63)
        global_row = row * FR + key_row - 3
        global_col = seq * FC + key_col
        inside = (global_row >= 0) & (global_row < n_rows * FR)
        inside = inside & (global_col >= 0) & (global_col < n_seq * FC)
        inside = inside & (key_col - query_col >= -3) & (key_col - query_col <= 3)
        gap = jnp.where(inside, key_row, 1000)
        for r in range(2):
            for h in range(4):
                start = (r * 4 + h) * FC
                halo_gap[t, start : start + FC, :] = gap - r

    for i in range(4):
        attend_own(i)

    def attend(i):
        t = i // 2
        scores = lax.dot_general(
            stacked[i], halo_keys[t], last_dims, preferred_element_type=F32
        )
        off = halo_gap[t] - i * 2
        weights = jnp.where((off >= 0) & (off <= 6), jnp.exp2(scores * factors), 0.0)
        total = own_total[i] + dot(weights.astype(BF), halo_vals[t])
        weight_sum = jnp.sum(own_sum[i], axis=-1, keepdims=True) + jnp.sum(
            weights, axis=-1, keepdims=True
        )
        scaled = total * (1.0 / weight_sum)
        picked = []
        for r in range(2):
            parts = [scaled[(r * 4 + h) * FC : (r * 4 + h + 1) * FC] for h in range(4)]
            merged_heads = parts[0]
            for h in range(1, 4):
                merged_heads = jnp.where(lane_head == h, parts[h], merged_heads)
            picked.append(merged_heads)
        attended[i * 128 : (i + 1) * 128, :] = jnp.concatenate(picked, axis=0).astype(BF)

    def end_rows(t, rows_here):
        kv = project(xpad[rows_here].reshape(3 * FC, FD), FD)
        halo_keys[t, SIDE:, :] = unit_bf(kv[:, :FD])
        halo_vals[t, SIDE:, :] = kv[:, FD:]

    hidden = w_ffn.shape[0]
    take = lax.broadcasted_iota(jnp.int32, (128, 128), 0)
    come = lax.broadcasted_iota(jnp.int32, (128, 128), 1)
    wanted = (take >> 6) * 64 + (take & 31) * 2 + ((take >> 5) & 1)
    permute = jnp.where(come == wanted, 1.0, 0.0).astype(BF)
    gain_f = gain_ffn[...]

    def feed(i):
        tokens = slice(i * 256, (i + 1) * 256)
        here = xpad[3 + 4 * i : 7 + 4 * i].reshape(256, FD).astype(F32)
        stream = here + dot(attended[tokens, :], w_proj[...])
        normed = rms(stream, gain_f)
        for c in range(0, hidden, 256):
            value = dot(normed, w_in[:, c : c + 256])
            gate = dot(normed, w_in[:, hidden + c : hidden + c + 256])
            gated = (value * jax.nn.gelu(gate)).astype(BF)
            stream = stream + dot(gated, w_ffn[c : c + 256, :])
        fine = stream.astype(BF)
        fine_out[tokens, :] = fine
        for j in range(2):
            part = dot(permute, fine[j * 128 : (j + 1) * 128]).astype(BF)
            start = (i * 2 + j) * 32
            merged[start : start + 32, :] = jnp.concatenate(
                [part[n * 32 : (n + 1) * 32] for n in range(4)], axis=1
            )

    low_half = lax.broadcasted_iota(jnp.int32, (HT, 128), 1) < HEAD
    copies = {}

    def exchange(t):
        tokens = slice(t * HT, (t + 1) * HT)
        coarse = dot(merged[tokens, :], w_merge[...]).astype(BF)
        coarse_in[tokens, :] = coarse
        normed = rms(coarse.astype(F32), gain_coarse[...])

        def heads(which):
            cols = slice(which * CD, (which + 1) * CD)
            return dot(normed, w_coarse[:, cols]).astype(BF).astype(F32)

        def unit_groups(values):
            return [unit(values[:, c : c + 256], blocks) for c in range(0, CD, 256)]

        def query_part():
            query = unit_groups(heads(0))
            for p in range(8):
                pair = query[p // 2][:, (p % 2) * 128 : (p % 2 + 1) * 128]
                turned = jnp.concatenate([pair, pair], axis=0).T
                for e in range(2):
                    first, second = turned[e * 64 : e * 64 + 32], turned[e * 64 + 32 : e * 64 + 64]
                    part = jnp.where(low_half[:32], first, second).astype(BF)
                    messages[t, 2 * p + e, HT:] = part

        def key_part():
            key = unit_groups(heads(1))
            value = heads(2)
            for p in range(8):
                k2 = key[p // 2][:, (p % 2) * 128 : (p % 2 + 1) * 128]
                v2 = value[:, p * 128 : (p + 1) * 128]
                even = jnp.where(low_half, k2, pltpu.roll(v2, HEAD, 1))
                odd = jnp.where(low_half, pltpu.roll(k2, HEAD, 1), v2)
                messages[t, 2 * p, :HT] = even.astype(BF)
                messages[t, 2 * p + 1, :HT] = odd.astype(BF)

        def send(name, rows_here, target):
            for k in farthest:
                dy, dz = partners[k]
                their_head = lax.rem(y + dy, 4) * 4 + lax.rem(z + dz, 4)
                copies[name, k] = remote(
                    messages.at[t, their_head, rows_here],
                    target(k),
                    x_send.at[name, k],
                    x_recv.at[name, k],
                    at(dy, dz),
                )
                copies[name, k].start()

        if t == 0:
            query_part()
            key_part()
            send(0, pl.ds(0, 96), lambda k: landed.at[k])
        else:
            query_part()
            send(1, pl.ds(HT, 32), lambda k: q_buf.at[k])
            key_part()
            send(2, pl.ds(0, HT), lambda k: kv_buf.at[2, pl.ds(k * HT, HT)])
            kv_buf[2, own * HT : (own + 1) * HT, :] = messages[1, head, :HT]

    for place in halo:
        if place != (1, 0) and place != (-1, 0):
            halo[place].wait()
    side_kv = project(side[...].reshape(SIDE, FD), FD)
    side_keys = unit_bf(side_kv[:, :FD])
    for t in range(2):
        halo_keys[t, :SIDE, :] = side_keys
        halo_vals[t, :SIDE, :] = side_kv[:, FD:]
    halo[1, 0].wait()
    end_rows(0, slice(0, 3))
    attend(0)
    attend(1)
    w_proj_load.wait()
    w_in_load.wait()
    w_ffn_load.wait()
    feed(0)
    w_merge_load.wait()
    w_coarse_load.wait()
    exchange(0)
    halo[-1, 0].wait()
    end_rows(1, slice(FR + 3, FR + 6))
    attend(2)
    attend(3)
    feed(1)
    exchange(1)

    q_full[HEAD:, :] = jnp.zeros((HEAD, QUERIES), BF)
    acc[...] = jnp.zeros_like(acc)
    def gather(source, target, there):
        return remote(
            kv_buf.at[source], kv_buf.at[target], g_send.at[target], g_recv.at[target], there
        )

    gathers = {
        1: gather(0, 1, sibling),
        3: gather(2, 3, sibling),
        4: gather(0, 4, up),
        5: gather(0, 5, down),
        6: gather(4, 6, sibling),
        7: gather(5, 7, sibling),
        8: gather(2, 8, up),
        9: gather(2, 9, down),
        10: gather(8, 10, sibling),
        11: gather(9, 11, sibling),
        12: gather(4, 12, up),
        13: gather(9, 13, down),
        14: gather(12, 14, sibling),
        15: gather(13, 15, sibling),
    }
    arrive = {b: ("gather", (b,)) for b in gathers}
    arrive[0] = ("plane", [(0, k) for k in range(16)])
    arrive[2] = ("plane", [(2, k) for k in range(16)])
    arrive[8] = ("gather", (8, 9))
    arrive[12] = ("gather", (12, 13))
    del arrive[9], arrive[13]
    start_after = {0: (1, 4, 5), 2: (3, 8, 9), 4: (6, 12), 5: (7,), 8: (10, 11, 13), 12: (14, 15)}

    def arrivals(b):
        kind, which = arrive[b]
        for k in which:
            if kind == "gather":
                gathers[k].wait_recv()
            elif k[1] != own:
                copies[k].wait()
        if b == 0:
            for k in range(16):
                part = messages[0, head, :HT] if k == own else landed[k, :HT]
                kv_buf[0, k * HT : (k + 1) * HT, :] = part
        for target in start_after.get(b, ()):
            gathers[target].start()

    def assemble(t):
        for k in range(0, 16, 2):
            parts = []
            for j in (k, k + 1):
                if j == own:
                    part = messages[t, head, HT:]
                elif t == 0:
                    part = landed[j, HT:]
                else:
                    copies[1, j].wait()
                    part = q_buf[j]
                parts.append(part.astype(F32))
            top = jnp.where(low_half[:32], parts[0], pltpu.roll(parts[1], HEAD, 1))
            end = jnp.where(low_half[:32], pltpu.roll(parts[0], HEAD, 1), parts[1])
            cols = slice(t * half + k * HT, t * half + (k + 2) * HT)
            q_full[0:HEAD, cols] = jnp.concatenate([top, end], axis=0).astype(BF)

    o_copies = {}
    half, quarter = QUERIES // 2, QUERIES // 4
    of_head = lax.broadcasted_iota(jnp.int32, (1, NHEAD), 1) == head
    head_scale = jnp.sum(jnp.where(of_head, scale_coarse[...], 0.0), axis=1, keepdims=True)
    head_factor = head_scale * (LOG2E / HEAD)
    ones = jnp.ones((8, BLOCK), BF)

    def process(b, parts):
        kv = kv_buf[b]
        lhs = jnp.concatenate([kv.T[HEAD:], ones], axis=0)
        for cols in parts:
            weights = jnp.exp2(dot(kv, q_full[:, cols]) * head_factor).astype(BF)
            acc[:, cols] += dot(lhs, weights)

    all_parts = [slice(i * quarter, (i + 1) * quarter) for i in range(4)]

    arrivals(0)
    assemble(0)
    process(0, all_parts[:2])
    arrivals(1)
    process(1, all_parts[:2])
    assemble(1)

    def step(i, carry):
        @pl.when(i < 2)
        def _():
            process(i, all_parts[2:])

        @pl.when(i >= 2)
        def _():
            for block in sorted(arrive):
                if 1 < block < 12:
                    pl.when(i == block)(lambda block=block: arrivals(block))
            process(i, [slice(0, half), slice(half, QUERIES)])

        return carry

    lax.fori_loop(0, 12, step, 0)

    low_rows = lax.broadcasted_iota(jnp.int32, (HEAD, 128), 1) < HEAD
    for first in (0, 1):
        parts = [all_parts[first], all_parts[first + 2]]

        def last(i, carry):
            if first == 0:
                pl.when(i == 0)(lambda: arrivals(12))

                @pl.when(i == 2)
                def _():
                    arrivals(14)
                    arrivals(15)

            process(12 + i, parts)
            return carry

        lax.fori_loop(0, 4, last, 0)
        done = [acc[0:HEAD, cols] * (1.0 / acc[HEAD : HEAD + 1, cols]) for cols in parts]
        for k in range(first * 8, first * 8 + 8, 2):
            start = (k - first * 8) * HT
            early, late = (half_done[:, start : start + 128] for half_done in done)
            both = (
                jnp.where(low_rows, early, pltpu.roll(late, HEAD, 1)).astype(BF),
                jnp.where(low_rows, pltpu.roll(early, HEAD, 1), late).astype(BF),
            )
            for j in (k, k + 1):
                if j == own:
                    back[head] = both[j - k]
                    continue
                dy, dz = partners[j]
                o_buf[j] = both[j - k]
                o_copies[j] = remote(
                    o_buf.at[j], back.at[head], o_send.at[j], o_recv.at[j], at(-dy, -dz)
                )
                o_copies[j].start()

    for copy in gathers.values():
        copy.wait_send()
    w_out_load.wait()
    total = coarse_in[...].astype(F32)
    for n, dy in enumerate(ORDER):
        for dz in range(4):
            if n * 4 + dz != own:
                o_copies[n * 4 + dz].wait()
        from_y = lax.rem(y + dy, 4)
        features = back[pl.ds(from_y * 4, 4)].reshape(256, CT)
        rows_here = pl.ds(pl.multiple_of(from_y * 256, 256), 256)
        total = total + lax.dot_general(
            features, w_out[rows_here, :], (((0,), (0,)), ((), ())), preferred_element_type=F32
        )
    out[...] = total.astype(BF)


def body(
    image,
    gain_attn,
    w_qkv_fine,
    scale_fine,
    w_out_fine,
    gain_ffn,
    w_ffn_in,
    w_ffn_out,
    w_merge,
    gain_coarse,
    w_qkv_coarse,
    scale_coarse,
    w_out_coarse,
):
    vmem = pl.BlockSpec(memory_space=pltpu.VMEM)
    hbm = pl.BlockSpec(memory_space=pl.ANY)
    dma = pltpu.SemaphoreType.DMA
    weights = (w_qkv_fine, w_out_fine, w_ffn_in, w_ffn_out, w_merge, w_qkv_coarse, w_out_coarse)
    fine_out, coarse_out = pl.pallas_call(
        kernel,
        out_shape=(pltpu.VMEM((FR * FC, FD), BF), pltpu.VMEM((CT, CD), BF)),
        in_specs=[hbm] * 13,
        out_specs=(vmem, vmem),
        scratch_shapes=[
            pltpu.VMEM((PR, FC, FD), BF),
            pltpu.VMEM((64, FD), BF),
            pltpu.VMEM((2, 64, FD), BF),
            pltpu.VMEM((OWN, FD), BF),
            pltpu.VMEM((OWN, FD), BF),
            pltpu.VMEM((2, HALO, FD), BF),
            pltpu.VMEM((2, HALO, FD), BF),
            pltpu.VMEM((4 * FC, OWN), F32),
            pltpu.VMEM((2, 8 * FC, HALO), jnp.int32),
            pltpu.VMEM((4, 8 * FC, FD), BF),
            pltpu.VMEM((4, 8 * FC, FD), F32),
            pltpu.VMEM((4, 8 * FC, 128), F32),
            pltpu.VMEM((FR * FC, FD), BF),
            pltpu.VMEM((CT, CD), BF),
            pltpu.VMEM((CT, CD), BF),
            pltpu.VMEM((2, NHEAD, HT + HEAD // 2, 128), BF),
            pltpu.VMEM((NHEAD, HT + HEAD // 2, 128), BF),
            pltpu.VMEM((NBLOCK, BLOCK, 128), BF),
            pltpu.VMEM((NHEAD, HEAD // 2, 128), BF),
            pltpu.VMEM((128, QUERIES), BF),
            pltpu.VMEM((HEAD + 8, QUERIES), F32),
            pltpu.VMEM((NHEAD, HEAD, CT), BF),
            pltpu.VMEM((NHEAD, HEAD, CT), BF),
        ]
        + [pltpu.VMEM(w.shape, BF) for w in weights]
        + [pltpu.VMEM((1, n), F32) for n in (FD, FD, CD, 4, NHEAD)]
        + [dma((13,)), dma((8,)), dma((8,))]
        + [dma((3, 16))] * 2
        + [dma((16,))] * 4,
        compiler_params=pltpu.CompilerParams(
            collective_id=0, has_side_effects=True, vmem_limit_bytes=VMEM_LIMIT
        ),
        name="window",
    )(
        image,
        gain_attn.reshape(1, -1),
        w_qkv_fine,
        scale_fine.reshape(1, -1),
        w_out_fine,
        gain_ffn.reshape(1, -1),
        w_ffn_in,
        w_ffn_out,
        w_merge,
        gain_coarse.reshape(1, -1),
        w_qkv_coarse,
        scale_coarse.reshape(1, -1),
        w_out_coarse,
    )
    return fine_out.reshape(image.shape), coarse_out.reshape(FR // 2, FC // 2, CD)


def solution(mesh):
    placed = (P("rows", "seq", None),) + (P(),) * 12
    return jax.shard_map(
        body,
        mesh=mesh,
        in_specs=placed,
        out_specs=(P("rows", "seq", None), P("rows", "seq", None)),
        check_vma=False,
    )
```

```python
import math

import jax
import jax.numpy as jnp
from jax import lax
from jax.experimental import pallas as pl
from jax.experimental.pallas import tpu as pltpu
from jax.sharding import PartitionSpec as P

HEAD = 64
MESH = pl.DeviceIdType.MESH
BF = jnp.bfloat16
F32 = jnp.float32
LOG2E = math.log2(math.e)

FR, FC, FD = 8, 64, 256
PR = FR + 6
OWN = FR * FC
SIDE = 128
HALO = SIDE + 3 * FC
CT, CD = 128, 1024
NHEAD = 16
HT = CT // 2
QUERIES = NHEAD * CT
BLOCK = 1024
NBLOCK = 16
ORDER = (1, 2, 3, 0)
VMEM_LIMIT = 56 * 2**20


def rms(values, gain):
    mean_square = jnp.mean(values * values, axis=-1, keepdims=True)
    return (values * lax.rsqrt(mean_square + 1e-06) * gain).astype(BF)


def dot(a, b):
    return jnp.dot(a, b, preferred_element_type=F32)


def unit(values, blocks):
    square = values * values
    high = square.astype(BF)
    low = (square - high.astype(F32)).astype(BF)
    return values * lax.rsqrt(dot(high, blocks) + dot(low, blocks) + 1e-06)


def kernel(
    image,
    gain_attn_hbm,
    w_qkv_hbm,
    scale_fine_hbm,
    w_proj_hbm,
    gain_ffn_hbm,
    w_in_hbm,
    w_ffn_hbm,
    w_merge_hbm,
    gain_coarse_hbm,
    w_coarse_hbm,
    scale_coarse_hbm,
    w_out_hbm,
    fine_out,
    out,
    xpad,
    packed,
    side,
    keys,
    vals,
    halo_keys,
    halo_vals,
    bias,
    halo_gap,
    stacked,
    own_total,
    own_sum,
    attended,
    merged,
    coarse_in,
    messages,
    landed,
    kv_buf,
    q_buf,
    q_full,
    acc,
    o_buf,
    back,
    w_qkv,
    w_proj,
    w_in,
    w_ffn,
    w_merge,
    w_coarse,
    w_out,
    gain_attn,
    gain_ffn,
    gain_coarse,
    scale_fine,
    scale_coarse,
    load_sem,
    halo_send,
    halo_recv,
    x_send,
    x_recv,
    g_send,
    g_recv,
    o_send,
    o_recv,
):
    row, seq = lax.axis_index("rows"), lax.axis_index("seq")
    n_rows, n_seq = lax.axis_size("rows"), lax.axis_size("seq")
    x, y, z_lo = row // 8, lax.rem(row // 2, 4), lax.rem(row, 2)
    z_hi, core = seq // 2, lax.rem(seq, 2)
    z = z_hi * 2 + z_lo
    head = y * 4 + z

    def at(dy, dz):
        py, pz = lax.rem(y + dy + 4, 4), lax.rem(z + dz + 4, 4)
        return (x * 8 + py * 2 + lax.rem(pz, 2), (pz // 2) * 2 + core)

    def beside(dr, ds):
        return (lax.rem(row + dr + n_rows, n_rows), lax.rem(seq + ds + n_seq, n_seq))

    sibling = (row, seq + 1 - 2 * core)
    up = (lax.rem(row + 8, 32), seq)
    down = (lax.rem(row + 24, 32), seq)
    around = [(dr, ds) for dr in (0, -1, 1) for ds in (0, -1, 1) if (dr, ds) != (0, 0)]
    partners = [(dy, dz) for dy in ORDER for dz in range(4)]
    own = partners.index((0, 0))
    hops = (0, 1, 2, 1)
    farthest = sorted(range(16), key=lambda k: -hops[partners[k][0]] - hops[partners[k][1]])
    farthest.remove(own)

    def load(source, target, i):
        copy = pltpu.make_async_copy(source, target, load_sem.at[i])
        copy.start()
        return copy

    image_load = load(image, xpad.at[pl.ds(3, FR)], 0)
    barrier = pltpu.get_barrier_semaphore()
    everyone = [beside(dr, ds) for dr, ds in around]
    everyone += [at(dy, dz) for k, (dy, dz) in enumerate(partners) if k != own]
    everyone += [sibling, up, down]
    for there in everyone:
        pl.semaphore_signal(barrier, inc=1, device_id=there, device_id_type=MESH)

    w_qkv_load = load(w_qkv_hbm, w_qkv, 1)
    small_loads = [
        load(gain_attn_hbm, gain_attn, 8),
        load(gain_ffn_hbm, gain_ffn, 9),
        load(gain_coarse_hbm, gain_coarse, 10),
        load(scale_fine_hbm, scale_fine, 11),
        load(scale_coarse_hbm, scale_coarse, 12),
    ]
    w_proj_load = load(w_proj_hbm, w_proj, 2)
    w_in_load = load(w_in_hbm, w_in, 3)
    w_ffn_load = load(w_ffn_hbm, w_ffn, 4)
    w_merge_load = load(w_merge_hbm, w_merge, 5)
    w_coarse_load = load(w_coarse_hbm, w_coarse, 6)
    w_out_load = load(w_out_hbm, w_out, 7)

    def remote(src, dst, send, recv, there):
        return pltpu.make_async_remote_copy(
            src_ref=src,
            dst_ref=dst,
            send_sem=send,
            recv_sem=recv,
            device_id=there,
            device_id_type=MESH,
        )

    image_load.wait()
    pl.semaphore_wait(barrier, len(everyone))

    halo = {}

    def send_halo(place, source, target):
        i = len(halo)
        halo[place] = remote(source, target, halo_send.at[i], halo_recv.at[i], beside(*place))
        halo[place].start()

    send_halo((1, 0), xpad.at[pl.ds(FR, 3)], xpad.at[pl.ds(0, 3)])
    take = lax.broadcasted_iota(jnp.int32, (64, FR * FC), 0)
    come = lax.broadcasted_iota(jnp.int32, (64, FR * FC), 1)
    wanted = ((take & 31) >> 2) * FC + (take & 3) + (take >> 5) * (FC - 4)
    pick = jnp.where(come == wanted, 1.0, 0.0).astype(BF)
    packed[...] = dot(pick, xpad[3 : 3 + FR].reshape(FR * FC, FD)).astype(BF)
    for ds, start in ((-1, 0), (1, 32)):
        there = 1 if ds == -1 else 0
        send_halo((0, ds), packed.at[pl.ds(start, 32)], side.at[there, pl.ds(16, 32)])
        send_halo((-1, ds), packed.at[pl.ds(start, 16)], side.at[there, pl.ds(48, 16)])
        send_halo((1, ds), packed.at[pl.ds(start + 16, 16)], side.at[there, pl.ds(0, 16)])
    send_halo((-1, 0), xpad.at[pl.ds(3, 3)], xpad.at[pl.ds(FR + 3, 3)])

    group = (lax.broadcasted_iota(jnp.int32, (FD, FD), 0) >> 6) == (
        lax.broadcasted_iota(jnp.int32, (FD, FD), 1) >> 6
    )
    blocks = jnp.where(group, 1.0 / HEAD, 0.0).astype(BF)
    w_qkv_load.wait()
    for copy in small_loads:
        copy.wait()
    gain = gain_attn[...]

    def project(tokens, first):
        normed = rms(tokens.astype(F32), gain)
        return dot(normed, w_qkv[:, first:]).astype(BF)

    def unit_bf(values):
        return unit(values.astype(F32), blocks).astype(BF)

    lane_head = lax.broadcasted_iota(jnp.int32, (FC, FD), 1) >> 6
    for i in range(2):
        tokens = slice(i * 256, (i + 1) * 256)
        triple = project(xpad[3 + 4 * i : 7 + 4 * i].reshape(256, FD), 0)
        query = unit(triple[:, :FD].astype(F32), blocks)
        for r in range(4):
            for h in range(4):
                one = jnp.where(lane_head == h, query[r * FC : (r + 1) * FC], 0.0)
                start = ((r % 2) * 4 + h) * FC
                stacked[i * 2 + r // 2, start : start + FC, :] = one.astype(BF)
        keys[tokens, :] = unit_bf(triple[:, FD : 2 * FD])
        vals[tokens, :] = triple[:, 2 * FD :]

    query_col = lax.broadcasted_iota(jnp.int32, (FC, OWN), 0)
    gap = (lax.broadcasted_iota(jnp.int32, (FC, OWN), 1) & 63) - query_col
    near = jnp.where((gap >= -3) & (gap <= 3), 0.0, -1e30).astype(F32)
    bias[...] = jnp.concatenate([near] * 4, axis=0)
    own_row = lax.broadcasted_iota(jnp.int32, (1, OWN), 1) >> 6
    factor = jnp.concatenate(
        [
            jnp.broadcast_to(scale_fine[0:1, h : h + 1] * (LOG2E / HEAD), (FC, 1))
            for h in range(4)
        ],
        axis=0,
    )
    factors = jnp.concatenate([factor, factor], axis=0)
    last_dims = (((1,), (1,)), ((), ()))

    def attend_own(i):
        scores = lax.dot_general(
            stacked[i], keys[...], last_dims, preferred_element_type=F32
        )
        weights = []
        for r in range(2):
            off = own_row + 3 - r - 2 * i
            row_bias = jnp.where((off >= 0) & (off <= 6), 0.0, -1e30).astype(F32)
            part = scores[r * 256 : (r + 1) * 256] * factor + (bias[...] + row_bias)
            weights.append(jnp.exp2(part))
        weights = jnp.concatenate(weights, axis=0)
        own_total[i] = dot(weights.astype(BF), vals[...])
        weight_sum = weights[:, :128]
        for j in range(128, OWN, 128):
            weight_sum = weight_sum + weights[:, j : j + 128]
        own_sum[i] = weight_sum

    query_col = lax.broadcasted_iota(jnp.int32, (FC, HALO), 0)
    slot = lax.broadcasted_iota(jnp.int32, (FC, HALO), 1)
    beyond = slot - SIDE
    right = slot >> 6
    for t in range(2):
        key_row = jnp.where(slot < SIDE, ((slot & 63) >> 2) - 1, (beyond >> 6) + t * (FR + 3))
        key_col = jnp.where(slot < SIDE, (slot & 3) - 4 + right * (FC + 4), beyond & 63)
        global_row = row * FR + key_row - 3
        global_col = seq * FC + key_col
        inside = (global_row >= 0) & (global_row < n_rows * FR)
        inside = inside & (global_col >= 0) & (global_col < n_seq * FC)
        inside = inside & (key_col - query_col >= -3) & (key_col - query_col <= 3)
        gap = jnp.where(inside, key_row, 1000)
        for r in range(2):
            for h in range(4):
                start = (r * 4 + h) * FC
                halo_gap[t, start : start + FC, :] = gap - r

    for i in range(4):
        attend_own(i)

    def attend(i):
        t = i // 2
        scores = lax.dot_general(
            stacked[i], halo_keys[t], last_dims, preferred_element_type=F32
        )
        off = halo_gap[t] - i * 2
        weights = jnp.where((off >= 0) & (off <= 6), jnp.exp2(scores * factors), 0.0)
        total = own_total[i] + dot(weights.astype(BF), halo_vals[t])
        weight_sum = jnp.sum(own_sum[i], axis=-1, keepdims=True) + jnp.sum(
            weights, axis=-1, keepdims=True
        )
        scaled = total * (1.0 / weight_sum)
        picked = []
        for r in range(2):
            parts = [scaled[(r * 4 + h) * FC : (r * 4 + h + 1) * FC] for h in range(4)]
            merged_heads = parts[0]
            for h in range(1, 4):
                merged_heads = jnp.where(lane_head == h, parts[h], merged_heads)
            picked.append(merged_heads)
        attended[i * 128 : (i + 1) * 128, :] = jnp.concatenate(picked, axis=0).astype(BF)

    def end_rows(t, rows_here):
        kv = project(xpad[rows_here].reshape(3 * FC, FD), FD)
        halo_keys[t, SIDE:, :] = unit_bf(kv[:, :FD])
        halo_vals[t, SIDE:, :] = kv[:, FD:]

    hidden = w_ffn.shape[0]
    take = lax.broadcasted_iota(jnp.int32, (128, 128), 0)
    come = lax.broadcasted_iota(jnp.int32, (128, 128), 1)
    wanted = (take >> 6) * 64 + (take & 31) * 2 + ((take >> 5) & 1)
    permute = jnp.where(come == wanted, 1.0, 0.0).astype(BF)
    gain_f = gain_ffn[...]

    def feed(i):
        tokens = slice(i * 256, (i + 1) * 256)
        here = xpad[3 + 4 * i : 7 + 4 * i].reshape(256, FD).astype(F32)
        stream = here + dot(attended[tokens, :], w_proj[...])
        normed = rms(stream, gain_f)
        for c in range(0, hidden, 256):
            value = dot(normed, w_in[:, c : c + 256])
            gate = dot(normed, w_in[:, hidden + c : hidden + c + 256])
            gated = (value * jax.nn.gelu(gate)).astype(BF)
            stream = stream + dot(gated, w_ffn[c : c + 256, :])
        fine = stream.astype(BF)
        fine_out[tokens, :] = fine
        for j in range(2):
            part = dot(permute, fine[j * 128 : (j + 1) * 128]).astype(BF)
            start = (i * 2 + j) * 32
            merged[start : start + 32, :] = jnp.concatenate(
                [part[n * 32 : (n + 1) * 32] for n in range(4)], axis=1
            )

    low_half = lax.broadcasted_iota(jnp.int32, (HT, 128), 1) < HEAD
    copies = {}

    def exchange(t):
        tokens = slice(t * HT, (t + 1) * HT)
        coarse = dot(merged[tokens, :], w_merge[...]).astype(BF)
        coarse_in[tokens, :] = coarse
        normed = rms(coarse.astype(F32), gain_coarse[...])

        def heads(which):
            cols = slice(which * CD, (which + 1) * CD)
            return dot(normed, w_coarse[:, cols]).astype(BF).astype(F32)

        def unit_groups(values):
            return [unit(values[:, c : c + 256], blocks) for c in range(0, CD, 256)]

        def query_part():
            query = unit_groups(heads(0))
            for p in range(8):
                pair = query[p // 2][:, (p % 2) * 128 : (p % 2 + 1) * 128]
                turned = jnp.concatenate([pair, pair], axis=0).T
                for e in range(2):
                    first, second = turned[e * 64 : e * 64 + 32], turned[e * 64 + 32 : e * 64 + 64]
                    part = jnp.where(low_half[:32], first, second).astype(BF)
                    messages[t, 2 * p + e, HT:] = part

        def key_part():
            key = unit_groups(heads(1))
            value = heads(2)
            for p in range(8):
                k2 = key[p // 2][:, (p % 2) * 128 : (p % 2 + 1) * 128]
                v2 = value[:, p * 128 : (p + 1) * 128]
                even = jnp.where(low_half, k2, pltpu.roll(v2, HEAD, 1))
                odd = jnp.where(low_half, pltpu.roll(k2, HEAD, 1), v2)
                messages[t, 2 * p, :HT] = even.astype(BF)
                messages[t, 2 * p + 1, :HT] = odd.astype(BF)

        def send(name, rows_here, target):
            for k in farthest:
                dy, dz = partners[k]
                their_head = lax.rem(y + dy, 4) * 4 + lax.rem(z + dz, 4)
                copies[name, k] = remote(
                    messages.at[t, their_head, rows_here],
                    target(k),
                    x_send.at[name, k],
                    x_recv.at[name, k],
                    at(dy, dz),
                )
                copies[name, k].start()

        if t == 0:
            query_part()
            key_part()
            send(0, pl.ds(0, 96), lambda k: landed.at[k])
        else:
            query_part()
            send(1, pl.ds(HT, 32), lambda k: q_buf.at[k])
            key_part()
            send(2, pl.ds(0, HT), lambda k: kv_buf.at[2, pl.ds(k * HT, HT)])
            kv_buf[2, own * HT : (own + 1) * HT, :] = messages[1, head, :HT]

    for place in halo:
        if place != (1, 0) and place != (-1, 0):
            halo[place].wait()
    side_kv = project(side[...].reshape(SIDE, FD), FD)
    side_keys = unit_bf(side_kv[:, :FD])
    for t in range(2):
        halo_keys[t, :SIDE, :] = side_keys
        halo_vals[t, :SIDE, :] = side_kv[:, FD:]
    halo[1, 0].wait()
    end_rows(0, slice(0, 3))
    attend(0)
    attend(1)
    w_proj_load.wait()
    w_in_load.wait()
    w_ffn_load.wait()
    feed(0)
    w_merge_load.wait()
    w_coarse_load.wait()
    exchange(0)
    halo[-1, 0].wait()
    end_rows(1, slice(FR + 3, FR + 6))
    attend(2)
    attend(3)
    feed(1)
    exchange(1)

    q_full[HEAD:, :] = jnp.zeros((HEAD, QUERIES), BF)
    acc[...] = jnp.zeros_like(acc)
    def gather(source, target, there):
        return remote(
            kv_buf.at[source], kv_buf.at[target], g_send.at[target], g_recv.at[target], there
        )

    gathers = {
        1: gather(0, 1, sibling),
        3: gather(2, 3, sibling),
        4: gather(0, 4, up),
        5: gather(0, 5, down),
        6: gather(4, 6, sibling),
        7: gather(5, 7, sibling),
        8: gather(2, 8, up),
        9: gather(2, 9, down),
        10: gather(8, 10, sibling),
        11: gather(9, 11, sibling),
        12: gather(4, 12, up),
        13: gather(9, 13, down),
        14: gather(12, 14, sibling),
        15: gather(13, 15, sibling),
    }
    arrive = {b: ("gather", (b,)) for b in gathers}
    arrive[0] = ("plane", [(0, k) for k in range(16)])
    arrive[2] = ("plane", [(2, k) for k in range(16)])
    arrive[8] = ("gather", (8, 9))
    arrive[12] = ("gather", (12, 13))
    del arrive[9], arrive[13]
    start_after = {0: (1, 4, 5), 2: (3, 8, 9), 4: (6, 12), 5: (7,), 8: (10, 11, 13), 12: (14, 15)}

    def arrivals(b):
        kind, which = arrive[b]
        for k in which:
            if kind == "gather":
                gathers[k].wait_recv()
            elif k[1] != own:
                copies[k].wait()
        if b == 0:
            for k in range(16):
                part = messages[0, head, :HT] if k == own else landed[k, :HT]
                kv_buf[0, k * HT : (k + 1) * HT, :] = part
        for target in start_after.get(b, ()):
            gathers[target].start()

    def assemble(t):
        for k in range(0, 16, 2):
            parts = []
            for j in (k, k + 1):
                if j == own:
                    part = messages[t, head, HT:]
                elif t == 0:
                    part = landed[j, HT:]
                else:
                    copies[1, j].wait()
                    part = q_buf[j]
                parts.append(part.astype(F32))
            top = jnp.where(low_half[:32], parts[0], pltpu.roll(parts[1], HEAD, 1))
            end = jnp.where(low_half[:32], pltpu.roll(parts[0], HEAD, 1), parts[1])
            cols = slice(t * half + k * HT, t * half + (k + 2) * HT)
            q_full[0:HEAD, cols] = jnp.concatenate([top, end], axis=0).astype(BF)

    o_copies = {}
    half, quarter = QUERIES // 2, QUERIES // 4
    of_head = lax.broadcasted_iota(jnp.int32, (1, NHEAD), 1) == head
    head_scale = jnp.sum(jnp.where(of_head, scale_coarse[...], 0.0), axis=1, keepdims=True)
    head_factor = head_scale * (LOG2E / HEAD)
    ones = jnp.ones((8, BLOCK), BF)

    def process(b, parts):
        kv = kv_buf[b]
        lhs = jnp.concatenate([kv.T[HEAD:], ones], axis=0)
        for cols in parts:
            weights = jnp.exp2(dot(kv, q_full[:, cols]) * head_factor).astype(BF)
            acc[:, cols] += dot(lhs, weights)

    all_parts = [slice(i * quarter, (i + 1) * quarter) for i in range(4)]

    arrivals(0)
    assemble(0)
    process(0, all_parts[:2])
    arrivals(1)
    process(1, all_parts[:2])
    assemble(1)

    def step(i, carry):
        @pl.when(i < 2)
        def _():
            process(i, all_parts[2:])

        @pl.when(i >= 2)
        def _():
            for block in sorted(arrive):
                if 1 < block < 12:
                    pl.when(i == block)(lambda block=block: arrivals(block))
            process(i, [slice(0, half), slice(half, QUERIES)])

        return carry

    lax.fori_loop(0, 12, step, 0)

    low_rows = lax.broadcasted_iota(jnp.int32, (HEAD, 128), 1) < HEAD
    for first in (0, 1):
        parts = [all_parts[first], all_parts[first + 2]]

        def last(i, carry):
            if first == 0:
                pl.when(i == 0)(lambda: arrivals(12))

                @pl.when(i == 2)
                def _():
                    arrivals(14)
                    arrivals(15)

            process(12 + i, parts)
            return carry

        lax.fori_loop(0, 4, last, 0)
        done = [acc[0:HEAD, cols] * (1.0 / acc[HEAD : HEAD + 1, cols]) for cols in parts]
        for k in range(first * 8, first * 8 + 8, 2):
            start = (k - first * 8) * HT
            early, late = (half_done[:, start : start + 128] for half_done in done)
            both = (
                jnp.where(low_rows, early, pltpu.roll(late, HEAD, 1)).astype(BF),
                jnp.where(low_rows, pltpu.roll(early, HEAD, 1), late).astype(BF),
            )
            for j in (k, k + 1):
                if j == own:
                    back[head] = both[j - k]
                    continue
                o_buf[j] = both[j - k]
        for j in farthest:
            if first * 8 <= j < first * 8 + 8:
                dy, dz = partners[j]
                o_copies[j] = remote(
                    o_buf.at[j], back.at[head], o_send.at[j], o_recv.at[j], at(-dy, -dz)
                )
                o_copies[j].start()

    for copy in gathers.values():
        copy.wait_send()
    w_out_load.wait()
    total = coarse_in[...].astype(F32)
    for n, dy in enumerate(ORDER):
        for dz in range(4):
            if n * 4 + dz != own:
                o_copies[n * 4 + dz].wait()
        from_y = lax.rem(y + dy, 4)
        features = back[pl.ds(from_y * 4, 4)].reshape(256, CT)
        rows_here = pl.ds(pl.multiple_of(from_y * 256, 256), 256)
        total = total + lax.dot_general(
            features, w_out[rows_here, :], (((0,), (0,)), ((), ())), preferred_element_type=F32
        )
    out[...] = total.astype(BF)


def body(
    image,
    gain_attn,
    w_qkv_fine,
    scale_fine,
    w_out_fine,
    gain_ffn,
    w_ffn_in,
    w_ffn_out,
    w_merge,
    gain_coarse,
    w_qkv_coarse,
    scale_coarse,
    w_out_coarse,
):
    vmem = pl.BlockSpec(memory_space=pltpu.VMEM)
    hbm = pl.BlockSpec(memory_space=pl.ANY)
    dma = pltpu.SemaphoreType.DMA
    weights = (w_qkv_fine, w_out_fine, w_ffn_in, w_ffn_out, w_merge, w_qkv_coarse, w_out_coarse)
    fine_out, coarse_out = pl.pallas_call(
        kernel,
        out_shape=(pltpu.VMEM((FR * FC, FD), BF), pltpu.VMEM((CT, CD), BF)),
        in_specs=[hbm] * 13,
        out_specs=(vmem, vmem),
        scratch_shapes=[
            pltpu.VMEM((PR, FC, FD), BF),
            pltpu.VMEM((64, FD), BF),
            pltpu.VMEM((2, 64, FD), BF),
            pltpu.VMEM((OWN, FD), BF),
            pltpu.VMEM((OWN, FD), BF),
            pltpu.VMEM((2, HALO, FD), BF),
            pltpu.VMEM((2, HALO, FD), BF),
            pltpu.VMEM((4 * FC, OWN), F32),
            pltpu.VMEM((2, 8 * FC, HALO), jnp.int32),
            pltpu.VMEM((4, 8 * FC, FD), BF),
            pltpu.VMEM((4, 8 * FC, FD), F32),
            pltpu.VMEM((4, 8 * FC, 128), F32),
            pltpu.VMEM((FR * FC, FD), BF),
            pltpu.VMEM((CT, CD), BF),
            pltpu.VMEM((CT, CD), BF),
            pltpu.VMEM((2, NHEAD, HT + HEAD // 2, 128), BF),
            pltpu.VMEM((NHEAD, HT + HEAD // 2, 128), BF),
            pltpu.VMEM((NBLOCK, BLOCK, 128), BF),
            pltpu.VMEM((NHEAD, HEAD // 2, 128), BF),
            pltpu.VMEM((128, QUERIES), BF),
            pltpu.VMEM((HEAD + 8, QUERIES), F32),
            pltpu.VMEM((NHEAD, HEAD, CT), BF),
            pltpu.VMEM((NHEAD, HEAD, CT), BF),
        ]
        + [pltpu.VMEM(w.shape, BF) for w in weights]
        + [pltpu.VMEM((1, n), F32) for n in (FD, FD, CD, 4, NHEAD)]
        + [dma((13,)), dma((8,)), dma((8,))]
        + [dma((3, 16))] * 2
        + [dma((16,))] * 4,
        compiler_params=pltpu.CompilerParams(
            collective_id=0, has_side_effects=True, vmem_limit_bytes=VMEM_LIMIT
        ),
        name="window",
    )(
        image,
        gain_attn.reshape(1, -1),
        w_qkv_fine,
        scale_fine.reshape(1, -1),
        w_out_fine,
        gain_ffn.reshape(1, -1),
        w_ffn_in,
        w_ffn_out,
        w_merge,
        gain_coarse.reshape(1, -1),
        w_qkv_coarse,
        scale_coarse.reshape(1, -1),
        w_out_coarse,
    )
    return fine_out.reshape(image.shape), coarse_out.reshape(FR // 2, FC // 2, CD)


def solution(mesh):
    placed = (P("rows", "seq", None),) + (P(),) * 12
    return jax.shard_map(
        body,
        mesh=mesh,
        in_specs=placed,
        out_specs=(P("rows", "seq", None), P("rows", "seq", None)),
        check_vma=False,
    )
```
